32 devices in a mesh: ctx: 4 (over y, x), pipe: 8 (over z, core).
Axes of the slice: x: 2, y: 2, z: 4, core: 2. Of those that a mesh axis runs over, the one named last changes fastest.
Arguments:
- q_in: bfloat16 [8, 1024, 128], P('pipe', 'ctx'), may hold values from -6 to 6
- k_in: bfloat16 [8, 1024, 128], P('pipe', 'ctx'), may hold values from -6 to 6
- v_in: bfloat16 [8, 1024, 1024], P('pipe', 'ctx'), may hold values from -6 to 6
- gate_in: bfloat16 [8, 1024, 1024], P('pipe', 'ctx'), may hold values from -6 to 6
- out_grad: bfloat16 [8, 1024, 1024], P('pipe', 'ctx'), may hold values from -6 to 6
- conv_weight: bfloat16 [8, 3, 1024], P('pipe'), may hold values from -3.5 to 3.5
- bounds: int32 [8, 4], P('pipe'), may hold values from 0 to 256, as said below
Outputs:
- q_grad: bfloat16 [8, 1024, 128], P('pipe', 'ctx')
- k_grad: bfloat16 [8, 1024, 128], P('pipe', 'ctx')
- v_grad: bfloat16 [8, 1024, 1024], P('pipe', 'ctx')
- gate_grad: bfloat16 [8, 1024, 1024], P('pipe', 'ctx')
The draws below stay inside these ranges and needn't reach their ends.
Inputs may be any that keep to these rules, and one draw needn't show every extreme that they name: bounds[s, c] is the offset within slice c of section s's sequence (of 256 tokens) at which a new document begins, or 256 where none begins at an offset of that slice; in slice 0 a document begins at offset 0 whatever bounds[s, 0] holds.
All inputs are finite; a program needn't handle non-finite values.
Results may differ from the reference program's by a relative error of at most 0.0015.
Values may be sent and summed in bfloat16 or wider, within the bound.
No kernel may reach another device: no remote copies, remote signals or barrier semaphores. Data moves between devices by JAX's collectives and lax.ppermute only.
A program may use at most 128 MiB of HBM per device.

```python
import jax
import jax.numpy as jnp
from jax import lax

HEADS = 8
F = 16
DV = 128
CONV = 3
TOK_DEV = 256
E = 273
SECTIONS = 8
SLICES = 4
TOKENS = 1024


def draw_bounds(key, part):
    first_key, second_key, third_key = jax.random.split(jax.random.fold_in(key, 17), 3)
    picks = jax.random.randint(first_key, (SECTIONS, SLICES), 0, 3 * TOK_DEV)
    offsets = jnp.minimum(picks, TOK_DEV)
    row_pick = jax.random.randint(second_key, (), 0, SECTIONS)
    col_pick = jax.random.randint(third_key, (), 0, SLICES)
    marked = (jnp.arange(SECTIONS)[:, None] == row_pick) & (jnp.arange(SLICES)[None, :] == col_pick)
    return jnp.where(marked, 0, offsets).astype(jnp.int32)


def steps_of(rng, extent, pieces, least, largest):
    level = 1.0
    for dim, shards_of in pieces:
        steps = jax.random.uniform(jax.random.fold_in(jax.random.fold_in(rng, 6), dim), (shards_of,), jnp.float32, least / len(pieces), largest / len(pieces))
        level = level * jnp.repeat(jnp.exp(steps), extent[dim] // shards_of).reshape((-1,) + (1,) * (len(extent) - 1 - dim))
    return level


def scatter_about(own_key, dims, deviation, most, shards=(), dtype=jnp.bfloat16):
    gain = steps_of(own_key, dims, shards, -0.22, 0.18) if shards else 1.0
    result = jax.random.normal(own_key, dims, jnp.float32) * deviation * gain
    return jnp.minimum(jnp.maximum(result, -most), most).astype(dtype)


def setup_inputs(seed: int = 0) -> dict:
    seeds = jax.random.split(jax.random.key(seed), 8)
    return {
        "q_in": scatter_about(seeds[0], (SECTIONS, TOKENS, HEADS * F), 1.0, 6.0, ((0, 8), (1, 4))),
        "k_in": scatter_about(seeds[1], (SECTIONS, TOKENS, HEADS * F), 1.0, 6.0, ((0, 8), (1, 4))),
        "v_in": scatter_about(seeds[2], (SECTIONS, TOKENS, HEADS * DV), 1.0, 6.0, ((0, 8), (1, 4))),
        "gate_in": scatter_about(seeds[3], (SECTIONS, TOKENS, HEADS * DV), 1.0, 6.0, ((0, 8), (1, 4))),
        "out_grad": scatter_about(seeds[4], (SECTIONS, TOKENS, HEADS * DV), 1.0, 6.0, ((0, 8), (1, 4))),
        "conv_weight": scatter_about(seeds[5], (SECTIONS, CONV, HEADS * DV), CONV ** -0.5, 3.5, ((0, 8),)),
        "bounds": draw_bounds(jax.random.fold_in(seeds[7], 71), 0),
    }


half_root = 0.7071067811865476
highest = lax.Precision.HIGHEST

def expand_features(inputs):
    width = inputs.shape[-1]
    outer = (inputs[..., :, None] * inputs[..., None, :]).reshape(inputs.shape[:-1] + (width * width,))
    ones_col = jnp.ones(inputs.shape[:-1] + (1,), jnp.float32)
    return jnp.concatenate([ones_col, inputs, outer * half_root], axis=-1)

def section_forward(q_in, k_in, v_in, gate_in, conv_weight, bounds):
    qk_scale = F ** (-0.25)
    queries = q_in.astype(jnp.float32).reshape(SLICES, TOK_DEV, HEADS, F) * qk_scale
    keys_scaled = k_in.astype(jnp.float32).reshape(SLICES, TOK_DEV, HEADS, F) * qk_scale
    values = v_in.astype(jnp.float32).reshape(SLICES, TOK_DEV, HEADS, DV)
    position = jnp.arange(TOK_DEV).astype(jnp.int32)

    def slice_step(carry, item):
        state, norm = carry
        query_block, key_block, value_block, boundary = item
        opening = boundary % TOK_DEV
        before_doc = (position < boundary).astype(jnp.float32)
        after_doc = (position >= opening).astype(jnp.float32)
        in_newdoc = position >= boundary
        causal_mask = (position[:, None] >= position[None, :]) & (in_newdoc[:, None] == in_newdoc[None, :])
        carried = (boundary == TOK_DEV).astype(jnp.float32)
        query_phi = expand_features(query_block)
        key_phi = expand_features(key_block)
        affine = jnp.einsum('thf,shf->hts', query_block, key_block, precision=highest)
        kernel = jnp.where(causal_mask[None], 1.0 + affine + 0.5 * affine * affine, 0.0)
        numerator = jnp.einsum('hts,shd->thd', kernel, value_block, precision=highest) + before_doc[:, None, None] * jnp.einsum('the,hed->thd', query_phi, state, precision=highest)
        denominator = lax.optimization_barrier(jnp.sum(kernel, axis=2)).T + before_doc[:, None] * jnp.einsum('the,he->th', query_phi, norm, precision=highest)
        attended = numerator / denominator[:, :, None]
        key_used = key_phi * after_doc[:, None, None]
        new_state = carried * state + jnp.einsum('the,thd->hed', key_used, value_block, precision=highest)
        new_norm = carried * norm + lax.optimization_barrier(jnp.sum(key_used, axis=0))
        return ((new_state, new_norm), attended)
    start_carry = (jnp.zeros((HEADS, E, DV), jnp.float32), jnp.zeros((HEADS, E), jnp.float32))
    final_carry, attended = lax.scan(slice_step, start_carry, (queries, keys_scaled, values, bounds))
    attended = attended.reshape(SLICES * TOK_DEV, HEADS * DV)
    flags = (bounds < TOK_DEV).astype(jnp.int32)
    running = jnp.cumsum(flags)
    doc_ids = (running[:, None] - flags[:, None] * (position[None, :] < bounds[:, None]).astype(jnp.int32)).reshape(SLICES * TOK_DEV)
    gate_rows = gate_in.astype(jnp.float32)
    taps = conv_weight.astype(jnp.float32)
    mixed = taps[0] * gate_rows
    for shift_by in range(1, CONV):
        moved = jnp.concatenate([jnp.zeros((shift_by, HEADS * DV), jnp.float32), gate_rows[:-shift_by]], axis=0)
        earlier_ids = jnp.concatenate([jnp.full((shift_by,), -1, jnp.int32), doc_ids[:-shift_by]], axis=0)
        same_doc = (earlier_ids == doc_ids).astype(jnp.float32)
        mixed = mixed + taps[shift_by] * moved * same_doc[:, None]
    return attended * jax.nn.silu(mixed)

def reference(q_in, k_in, v_in, gate_in, out_grad, conv_weight, bounds):
    incoming = jnp.roll(out_grad, -1, axis=0).astype(jnp.float32)

    def one_section(item):
        query_arg, key_arg, value_arg, gate_arg, cotangent, taps, section_bounds = item

        def forward(query_in, key_in, value_in, gate_value):
            return section_forward(query_in, key_in, value_in, gate_value, taps, section_bounds)
        primal, pullback = jax.vjp(forward, query_arg, key_arg, value_arg, gate_arg)
        return pullback(cotangent)
    grads = lax.map(one_section, (q_in, k_in, v_in, gate_in, incoming, conv_weight, bounds))
    return (jnp.roll(grads[0], -1, axis=0), jnp.roll(grads[1], -1, axis=0), jnp.roll(grads[2], -1, axis=0), jnp.roll(grads[3], -1, axis=0))
```

```python
import functools

import jax
import jax.numpy as jnp
from jax import lax
from jax.experimental import pallas as pl
from jax.experimental.pallas import tpu as pltpu
from jax.sharding import PartitionSpec as P

HEADS = 8
F = 16
DV = 128
CONV = 3
TOK = 256
ROWS = TOK + 2 * F
BF16 = jnp.bfloat16
F32 = jnp.float32
VMEM_LIMIT = 56 * 1024 * 1024

ANY = pl.BlockSpec(memory_space=pl.ANY)
SMEM = pl.BlockSpec(memory_space=pltpu.SMEM)
VMEM = pl.BlockSpec(memory_space=pltpu.VMEM)


def first_head(place, count):
    return (place * HEADS) // count


def phases_of(count):
    return max(1, HEADS // count)


def senders_of(count):
    return range(0, count, max(1, count // HEADS))


def pack_kernel(count, info, q_ref, k_ref, v_ref, gate_ref, grad_ref, *rest):
    phases = phases_of(count)
    blocks = phases * count
    packed, grads = rest[:blocks], rest[blocks : 2 * blocks]
    turned, sem, sem_turned = rest[2 * blocks :]
    me = info[0]
    copies = []
    for phase in range(phases):
        for partner in range(count):
            head = first_head(me ^ partner, count) + phase
            lanes = pl.ds(pl.multiple_of(head * DV, DV), DV)
            where = phase * count + partner
            out = packed[where]
            copies.append((v_ref.at[0, :, lanes], out.at[0:TOK, 0:DV]))
            copies.append((gate_ref.at[0, :, lanes], out.at[0:TOK, DV : 2 * DV]))
            copies.append((grad_ref.at[0, :, lanes], grads[where]))
    copies = [pltpu.make_async_copy(a, b, sem.at[n]) for n, (a, b) in enumerate(copies)]
    for copy in copies:
        copy.start()
    turned[0] = q_ref[0].astype(F32).T.astype(BF16)
    turned[1] = k_ref[0].astype(F32).T.astype(BF16)
    small = []
    for phase in range(phases):
        for partner in range(count):
            head = first_head(me ^ partner, count) + phase
            rows = pl.ds(pl.multiple_of(head * F, F), F)
            out = packed[phase * count + partner]
            for side in range(2):
                small.append((turned.at[side, rows], out.at[TOK + side * F : TOK + (side + 1) * F]))
    small = [pltpu.make_async_copy(a, b, sem_turned.at[n]) for n, (a, b) in enumerate(small)]
    for copy in small:
        copy.start()
    for copy in copies + small:
        copy.wait()


def pack(count, info, q_in, k_in, v_in, gate_in, grad):
    blocks = phases_of(count) * count
    out = pl.pallas_call(
        functools.partial(pack_kernel, count),
        out_shape=[jax.ShapeDtypeStruct((ROWS, 2 * DV), BF16)] * blocks
        + [jax.ShapeDtypeStruct((TOK, DV), BF16)] * blocks,
        in_specs=[SMEM, VMEM, VMEM, ANY, ANY, ANY],
        out_specs=[VMEM] * (2 * blocks),
        scratch_shapes=[
            pltpu.VMEM((2, HEADS * F, TOK), BF16),
            pltpu.SemaphoreType.DMA((3 * blocks,)),
            pltpu.SemaphoreType.DMA((2 * blocks,)),
        ],
        compiler_params=pltpu.CompilerParams(vmem_limit_bytes=VMEM_LIMIT),
    )(info, q_in, k_in, v_in, gate_in, grad)
    return out[:blocks], out[blocks:]


def nn(a, b):
    return lax.dot_general(a, b, (((1,), (0,)), ((), ())), preferred_element_type=F32)


def nt(a, b):
    return lax.dot_general(a, b, (((1,), (1,)), ((), ())), preferred_element_type=F32)


def halves(x):
    high = x.astype(BF16)
    return high, (x - high.astype(F32)).astype(BF16)


def iota(shape, dim):
    return lax.broadcasted_iota(jnp.int32, shape, dim)


def each(low, high, body):
    if isinstance(low, int) and isinstance(high, int) and high - low <= 4:
        for step in range(low, high):
            body(step)
    else:

        def one(step, carry):
            body(step)
            return carry

        lax.fori_loop(low, high, one, 0)


def attend_kernel(count, phase, info, taps_ref, *rest):
    senders = senders_of(count)
    packed, grads = rest[:count], rest[count : 2 * count]
    outs = rest[2 * count : 2 * count + len(senders)]
    (block, grad, gates, mixed_grads, high_s, low_s, base_s, num_s, dq_s, dk_s, dv_s, stage,
     sem_in, sem_grad, sem_out) = rest[2 * count + len(senders) :]
    me = info[0]
    arriving = []
    for partner in range(count):
        arriving.append(
            pltpu.make_async_copy(packed[partner], block.at[me ^ partner], sem_in.at[partner])
        )
        arriving.append(
            pltpu.make_async_copy(grads[partner], grad.at[me ^ partner], sem_grad.at[partner])
        )
    for copy in arriving:
        copy.start()
    head = first_head(me, count) + phase
    taps = taps_ref[0, :, pl.ds(pl.multiple_of(head * DV, DV), DV)].astype(F32)
    dk_s[...] = jnp.zeros_like(dk_s)
    dv_s[...] = jnp.zeros_like(dv_s)
    gates[0:8] = jnp.zeros((8, DV), F32)
    mixed_grads[:, count * TOK : count * TOK + 8] = jnp.zeros((CONV, 8, DV), F32)
    for copy in arriving:
        copy.wait()

    def spread(j):
        gates[pl.ds(8 + j * TOK, TOK)] = block[j, 0:TOK, DV : 2 * DV].astype(F32)

    each(0, count, spread)

    def opening(i):
        bound = info[1 + i]
        return jnp.where(bound < TOK, i * TOK + bound, 0)

    def earlier(i):
        if isinstance(i, int):
            last = jnp.int32(0)
            for j in range(i):
                last = jnp.maximum(last, opening(j))
            return last
        return lax.fori_loop(0, i, lambda j, last: jnp.maximum(last, opening(j)), jnp.int32(0))

    def doc_start(i, shape):
        token = iota(shape, 0)
        return jnp.where(token >= info[1 + i], opening(i), earlier(i))

    def row_block(i):
        bound = info[1 + i]
        before = earlier(i)
        in_old = iota((TOK, 2 * DV), 0) < bound
        in_old_lanes = iota((2 * DV, TOK), 1) < bound
        row, col = iota((TOK, TOK), 0), iota((TOK, TOK), 1)
        same = (col <= row) & ((col >= bound) | (row < bound))
        query_t = block[i, TOK : TOK + F] * BF16(0.25)
        query = query_t.astype(F32).T.astype(BF16)
        ones = jnp.ones((TOK, DV), BF16)

        def keys(j):
            return block[j, TOK + F : TOK + 2 * F]

        def kernel_of(j):
            base = 1.0 + nn(query, keys(j))
            return base, 0.5 * base * base + 0.5

        base, kern = kernel_of(i)
        high, low = halves(jnp.where(same, kern, 0.0))
        base_s[i] = base
        high_s[i] = high
        low_s[i] = low
        values_one = jnp.concatenate([block[i, 0:TOK, 0:DV], ones], axis=1)
        own = nn(high, values_one) + nn(low, values_one)
        num_s[...] = jnp.zeros_like(num_s)

        def forward(j):
            base, kern = kernel_of(j)
            high, low = halves(kern)
            base_s[j] = base
            high_s[j] = high
            low_s[j] = low
            values_one = jnp.concatenate([block[j, 0:TOK, 0:DV], ones], axis=1)
            values_one = jnp.where(
                iota((TOK, 2 * DV), 0) + j * TOK >= before, values_one.astype(F32), 0.0
            ).astype(BF16)
            num_s[...] += nn(high, values_one) + nn(low, values_one)

        each(0, i, forward)
        total = own + jnp.where(in_old, num_s[...], 0.0)
        num, den = total[:, 0:DV], total[:, DV:]

        position = iota((TOK, DV), 0) + i * TOK
        depth = position - doc_start(i, (TOK, DV))
        mixed = taps[0:1] * gates[pl.ds(8 + i * TOK, TOK)]
        for shift in range(1, CONV):
            moved = gates[pl.ds(8 - shift + i * TOK, TOK)]
            mixed += jnp.where(depth >= shift, taps[shift : shift + 1] * moved, 0.0)
        incoming = grad[i].astype(F32)
        gate = 1.0 / (1.0 + jnp.exp(-mixed))
        attended = num / den
        d_num = incoming * mixed * gate / den
        d_den = -jnp.sum(d_num * attended, axis=1, keepdims=True)
        mixed_grad = incoming * attended * gate * (1.0 + mixed * (1.0 - gate))
        mixed_grads[0, pl.ds(i * TOK, TOK)] = mixed_grad
        for shift in range(1, CONV):
            mixed_grads[shift, pl.ds(i * TOK, TOK)] = jnp.where(depth >= shift, mixed_grad, 0.0)
        d_high, d_low = halves(d_num)
        d_pair = jnp.concatenate([d_high, d_low], axis=1)
        d_pair_f32 = d_pair.astype(F32)
        d_pair_t = d_pair_f32.T
        d_pair_old = jnp.where(in_old, d_pair_f32, 0.0).astype(BF16)
        d_pair_old_t = jnp.where(in_old_lanes, d_pair_t, 0.0).astype(BF16)
        d_pair_t = d_pair_t.astype(BF16)
        d_den_old = jnp.where(iota((TOK, 1), 0) < bound, d_den, 0.0)

        def twice(j):
            value = block[j, 0:TOK, 0:DV]
            return jnp.concatenate([value, value], axis=1)

        slope = (nt(d_pair, twice(i)) + d_den) * base_s[i]
        s_high, s_low = halves(jnp.where(same, slope, 0.0))
        dv_s[i] += nn(d_pair_t, high_s[i]) + nn(d_pair_t, low_s[i])
        dk_s[i] += nn(query_t, s_high) + nn(query_t, s_low)
        dq_s[i] = nt(keys(i), s_high) + nt(keys(i), s_low)

        def backward(j):
            allowed = iota((TOK, TOK), 1) + j * TOK >= before
            slope = (nt(d_pair_old, twice(j)) + d_den_old) * base_s[j]
            s_high, s_low = halves(jnp.where(allowed, slope, 0.0))
            dv_s[j] += jnp.where(
                allowed, nn(d_pair_old_t, high_s[j]) + nn(d_pair_old_t, low_s[j]), 0.0
            )
            dk_s[j] += nn(query_t, s_high) + nn(query_t, s_low)
            dq_s[i] += nt(keys(j), s_high) + nt(keys(j), s_low)

        each(0, i, backward)

    each(0, count, row_block)

    def finish(j):
        total = dv_s[j, 0:DV] + dv_s[j, DV : 2 * DV]
        stage[j, 0:TOK, 0:DV] = total.T.astype(BF16)
        back = taps[0:1] * mixed_grads[0, pl.ds(j * TOK, TOK)]
        for shift in range(1, CONV):
            back += taps[shift : shift + 1] * mixed_grads[shift, pl.ds(j * TOK + shift, TOK)]
        stage[j, 0:TOK, DV : 2 * DV] = back.astype(BF16)
        stage[j, TOK : TOK + F] = (0.25 * dq_s[j]).astype(BF16)
        stage[j, TOK + F : TOK + 2 * F] = dk_s[j].astype(BF16)

    each(0, count, finish)
    leaving = [
        pltpu.make_async_copy(stage.at[me ^ partner], out, sem_out.at[n])
        for n, (partner, out) in enumerate(zip(senders, outs))
    ]
    for copy in leaving:
        copy.start()
    for copy in leaving:
        copy.wait()


def attend(count, phase, info, taps, packed, grads):
    outs = len(senders_of(count))
    return pl.pallas_call(
        functools.partial(attend_kernel, count, phase),
        out_shape=[jax.ShapeDtypeStruct((ROWS, 2 * DV), BF16)] * outs,
        in_specs=[SMEM, VMEM] + [ANY] * (2 * count),
        out_specs=[ANY] * outs,
        scratch_shapes=[
            pltpu.VMEM((count, ROWS, 2 * DV), BF16),
            pltpu.VMEM((count, TOK, DV), BF16),
            pltpu.VMEM((count * TOK + 8, DV), F32),
            pltpu.VMEM((CONV, count * TOK + 8, DV), F32),
            pltpu.VMEM((count, TOK, TOK), BF16),
            pltpu.VMEM((count, TOK, TOK), BF16),
            pltpu.VMEM((count, TOK, TOK), F32),
            pltpu.VMEM((TOK, 2 * DV), F32),
            pltpu.VMEM((count, F, TOK), F32),
            pltpu.VMEM((count, F, TOK), F32),
            pltpu.VMEM((count, 2 * DV, TOK), F32),
            pltpu.VMEM((count, ROWS, 2 * DV), BF16),
            pltpu.SemaphoreType.DMA((count,)),
            pltpu.SemaphoreType.DMA((count,)),
            pltpu.SemaphoreType.DMA((outs,)),
        ],
        compiler_params=pltpu.CompilerParams(vmem_limit_bytes=VMEM_LIMIT),
    )(info, taps, *packed, *grads)


def unpack_kernel(count, info, *rest):
    phases, senders = phases_of(count), senders_of(count)
    blocks = phases * len(senders)
    arrived = rest[:blocks]
    q_ref, k_ref, v_ref, gate_ref, turned, sem, sem_turned = rest[blocks:]
    me = info[0]
    copies, small = [], []
    for phase in range(phases):
        for n, partner in enumerate(senders):
            block = arrived[phase * len(senders) + n]
            head = first_head(me ^ partner, count) + phase
            lanes = pl.ds(pl.multiple_of(head * DV, DV), DV)
            rows = pl.ds(pl.multiple_of(head * F, F), F)
            for side in range(2):
                small.append(
                    (block.at[TOK + side * F : TOK + (side + 1) * F], turned.at[side, rows])
                )
            copies.append((block.at[0:TOK, 0:DV], v_ref.at[0, :, lanes]))
            copies.append((block.at[0:TOK, DV : 2 * DV], gate_ref.at[0, :, lanes]))
    small = [pltpu.make_async_copy(a, b, sem_turned.at[n]) for n, (a, b) in enumerate(small)]
    copies = [pltpu.make_async_copy(a, b, sem.at[n]) for n, (a, b) in enumerate(copies)]
    for copy in small + copies:
        copy.start()
    for copy in small:
        copy.wait()
    q_ref[0] = turned[0].astype(F32).T.astype(BF16)
    k_ref[0] = turned[1].astype(F32).T.astype(BF16)
    for copy in copies:
        copy.wait()


def unpack(count, info, arrived):
    blocks = len(arrived)
    return pl.pallas_call(
        functools.partial(unpack_kernel, count),
        out_shape=[jax.ShapeDtypeStruct((1, TOK, HEADS * F), BF16)] * 2
        + [jax.ShapeDtypeStruct((1, TOK, HEADS * DV), BF16)] * 2,
        in_specs=[SMEM] + [ANY] * blocks,
        out_specs=[VMEM] * 4,
        scratch_shapes=[
            pltpu.VMEM((2, HEADS * F, TOK), BF16),
            pltpu.SemaphoreType.DMA((2 * blocks,)),
            pltpu.SemaphoreType.DMA((2 * blocks,)),
        ],
        compiler_params=pltpu.CompilerParams(vmem_limit_bytes=VMEM_LIMIT),
    )(info, *arrived)


def on_device(count, sections, q_in, k_in, v_in, gate_in, out_grad, conv_weight, bounds):
    me = lax.axis_index("ctx")
    info = jnp.concatenate([me.astype(jnp.int32)[None], bounds[0]])
    phases, senders = phases_of(count), senders_of(count)

    def across(value, partner):
        if partner == 0:
            return value
        return lax.ppermute(value, "ctx", [(c, c ^ partner) for c in range(count)])

    def across_back(value, partner):
        pairs = [
            (c * sections + s, (c ^ partner) * sections + (s - 1) % sections)
            for c in range(count)
            for s in range(sections)
        ]
        return lax.ppermute(value, ("ctx", "pipe"), pairs)

    packed, grads = pack(count, info, q_in, k_in, v_in, gate_in, out_grad)
    arrived = []
    for phase in range(phases):
        mine = packed[phase * count : (phase + 1) * count]
        theirs = grads[phase * count : (phase + 1) * count]
        mine = [across(block, partner) for partner, block in enumerate(mine)]
        theirs = [across_back(block, partner) for partner, block in enumerate(theirs)]
        results = attend(count, phase, info, conv_weight, mine, theirs)
        arrived += [across_back(block, partner) for partner, block in zip(senders, results)]
    return tuple(unpack(count, info, arrived))


def solution(mesh):
    count, sections = mesh.shape["ctx"], mesh.shape["pipe"]
    split = P("pipe", "ctx", None)
    in_specs = (split,) * 5 + (P("pipe", None, None), P("pipe", None))
    return jax.shard_map(
        functools.partial(on_device, count, sections),
        mesh=mesh,
        in_specs=in_specs,
        out_specs=(split,) * 4,
        check_vma=False,
    )
```

```python
import functools

import jax
import jax.numpy as jnp
from jax import lax
from jax.experimental import pallas as pl
from jax.experimental.pallas import tpu as pltpu
from jax.sharding import PartitionSpec as P

HEADS = 8
F = 16
DV = 128
CONV = 3
TOK = 256
ROWS = TOK + 2 * F
BF16 = jnp.bfloat16
F32 = jnp.float32
UNROLLED = 4
HBM = pl.BlockSpec(memory_space=pltpu.HBM)

ANY = pl.BlockSpec(memory_space=pl.ANY)
SMEM = pl.BlockSpec(memory_space=pltpu.SMEM)
VMEM = pl.BlockSpec(memory_space=pltpu.VMEM)


def params(count):
    return pltpu.CompilerParams(vmem_limit_bytes=(14 if count <= UNROLLED else 44) * 1024 * 1024)


PACK_PARAMS = pltpu.CompilerParams(vmem_limit_bytes=125 * 512 * 1024)


def first_head(place, count):
    return (place * HEADS) // count


def lanes_of(head, width):
    return pl.ds(pl.multiple_of(head * width, width), width)


def phases_of(count):
    return max(1, HEADS // count)


def senders_of(count):
    return range(0, count, max(1, count // HEADS))


def pack_kernel(count, phase, q_ref, k_ref, v_ref, gate_ref, *rest):
    me = lax.axis_index("ctx")
    packed = rest[-4 - count : -4]
    rows, turned, sem, sem_rows = rest[-4:]
    copies = []
    for partner, out in enumerate(packed):
        lanes = lanes_of(first_head(me ^ partner, count) + phase, DV)
        copies.append((v_ref.at[0, :, lanes], out.at[0:TOK, 0:DV]))
        copies.append((gate_ref.at[0, :, lanes], out.at[0:TOK, DV : 2 * DV]))
    copies = [pltpu.make_async_copy(a, b, sem.at[n]) for n, (a, b) in enumerate(copies)]
    loads = [
        pltpu.make_async_copy(ref.at[0], rows.at[side], sem_rows.at[side])
        for side, ref in enumerate((q_ref, k_ref))
    ]
    for copy in loads + copies:
        copy.start()
    for side, copy in enumerate(loads):
        copy.wait()
        turned[side] = rows[side].astype(F32).T.astype(BF16)
    for partner, out in enumerate(packed):
        head = first_head(me ^ partner, count) + phase
        for side in range(2):
            mine = turned[side, lanes_of(head, F)]
            out[TOK + side * F : TOK + (side + 1) * F] = mine
    if phase > 0:
        grad_ref = rest[0]
        for partner, out in enumerate(packed):
            pack_grad(count, phase, me ^ partner, grad_ref, out)
    for copy in copies:
        copy.wait()


def pack_grad(count, phase, place, grad_ref, out):
    mine = grad_ref[0, :, lanes_of(first_head(place, count) + phase, DV)]
    half = TOK // 2
    base = 0 if phase == 0 else ROWS
    out[base : base + half, 0:DV] = mine[0:half]
    out[base : base + half, DV : 2 * DV] = mine[half:TOK]


def pack(count, phase, q_in, k_in, v_in, gate_in, *others):
    rows = ROWS if phase == 0 else ROWS + TOK // 2
    return pl.pallas_call(
        functools.partial(pack_kernel, count, phase),
        out_shape=[jax.ShapeDtypeStruct((rows, 2 * DV), BF16)] * count,
        in_specs=[HBM] * 4 + [VMEM] * min(1, len(others)) + [ANY] * max(0, len(others) - 1),
        out_specs=[VMEM] * count,
        scratch_shapes=[
            pltpu.VMEM((2, TOK, HEADS * F), BF16),
            pltpu.VMEM((2, HEADS * F, TOK), BF16),
            pltpu.SemaphoreType.DMA((2 * count,)),
            pltpu.SemaphoreType.DMA((2,)),
        ],
        compiler_params=PACK_PARAMS if phase == 0 else params(count),
    )(q_in, k_in, v_in, gate_in, *others)


def pack_grads_kernel(count, grad_ref, *outs):
    me = lax.axis_index("ctx")
    for partner, out in enumerate(outs):
        pack_grad(count, 0, me ^ partner, grad_ref, out)


def pack_grads(count, grad):
    return pl.pallas_call(
        functools.partial(pack_grads_kernel, count),
        out_shape=[jax.ShapeDtypeStruct((TOK // 2, 2 * DV), BF16)] * count,
        in_specs=[VMEM],
        out_specs=[VMEM] * count,
        compiler_params=params(count),
    )(grad)


def nn(a, b):
    return lax.dot_general(a, b, (((1,), (0,)), ((), ())), preferred_element_type=F32)


def nt(a, b):
    return lax.dot_general(a, b, (((1,), (1,)), ((), ())), preferred_element_type=F32)


def halves(x):
    high = x.astype(BF16)
    return high, (x - high.astype(F32)).astype(BF16)


def iota(shape, dim):
    return lax.broadcasted_iota(jnp.int32, shape, dim)


def each(low, high, body):
    if isinstance(low, int) and isinstance(high, int) and high - low <= UNROLLED:
        for step in range(low, high):
            body(step)
    else:

        def one(step, carry):
            body(step)
            return carry

        lax.fori_loop(low, high, one, 0)


def attend_kernel(count, phase, bounds, taps_ref, *rest):
    senders = senders_of(count)
    packed, rest = rest[:count], rest[count:]
    grads, base = packed, ROWS
    if phase == 0:
        grads, base, rest = rest[:count], 0, rest[count:]
    outs = rest[: len(senders)]
    (block, grad, gates, mixed_grads, high_s, low_s, base_s, num_s, dq_s, dk_s, dv_s,
    ) = rest[len(senders) :]
    me = lax.axis_index("ctx")
    for partner in range(count):
        block[me ^ partner] = packed[partner][0:ROWS]
        for half in range(2):
            grad[me ^ partner, half * TOK // 2 : (half + 1) * TOK // 2] = grads[partner][
                base : base + TOK // 2, half * DV : (half + 1) * DV
            ]
    head = first_head(me, count) + phase
    taps = taps_ref[0, :, pl.ds(pl.multiple_of(head * DV, DV), DV)].astype(F32)
    gates[0:8] = jnp.zeros((8, DV), F32)
    mixed_grads[:, count * TOK : count * TOK + 8] = jnp.zeros((CONV, 8, DV), F32)

    def spread(j):
        gates[pl.ds(8 + j * TOK, TOK)] = block[j, 0:TOK, DV : 2 * DV].astype(F32)

    each(0, count, spread)

    def opening(i):
        bound = bounds[0, i]
        return jnp.where(bound < TOK, i * TOK + bound, 0)

    def earlier(i):
        if isinstance(i, int):
            last = jnp.int32(0)
            for j in range(i):
                last = jnp.maximum(last, opening(j))
            return last
        return lax.fori_loop(0, i, lambda j, last: jnp.maximum(last, opening(j)), jnp.int32(0))

    def values(j, wide):
        return block[pl.ds(j, wide), 0:TOK, 0:DV].reshape(wide * TOK, DV)

    def keys(j, wide):
        parts = [block[j + step, TOK + F : TOK + 2 * F] for step in range(wide)]
        return parts[0] if wide == 1 else jnp.concatenate(parts, axis=1)

    def spans(i, body):
        if isinstance(i, int):
            if i > 0:
                body(0, i)
        else:
            each(0, i, lambda j: body(j, 1))

    def row_block(i):
        bound = bounds[0, i]
        before = earlier(i)
        row, col = iota((TOK, TOK), 0), iota((TOK, TOK), 1)
        same = (col <= row) & ((col >= bound) | (row < bound))
        query_t = block[i, TOK : TOK + F] * BF16(0.25)
        query = query_t.astype(F32).T.astype(BF16)

        def kernel_of(j, wide):
            base = 1.0 + nn(query, keys(j, wide))
            return base, 0.5 * base * base + 0.5

        def weigh(high, low, value):
            value = jnp.concatenate([value, jnp.ones_like(value)], axis=1)
            return nn(high, value) + nn(low, value)

        own_base, own_kern = kernel_of(i, 1)
        own_high, own_low = halves(jnp.where(same, own_kern, 0.0))
        own = weigh(own_high, own_low, values(i, 1))
        num_s[i] = jnp.zeros((TOK, 2 * DV), F32)
        room = (i * (i - 1)) // 2 * TOK if isinstance(i, int) else 0

        def forward(j, wide):
            width = wide * TOK
            base, kern = kernel_of(j, wide)
            high, low = halves(kern)
            lanes = pl.ds(room + j * TOK, width)
            base_s[:, lanes] = base
            high_s[:, lanes] = high
            low_s[:, lanes] = low
            value = values(j, wide)
            allowed = iota((width, DV), 0) + j * TOK >= before
            ones = jnp.where(allowed, 1.0, 0.0).astype(BF16)
            value = jnp.concatenate([value * ones, ones], axis=1)
            num_s[i] += nn(high, value) + nn(low, value)

        spans(i, forward)
        yield
        old = iota((TOK, 2 * DV), 0) < bound
        total = own + jnp.where(old, num_s[i], 0.0)
        num, den = total[:, 0:DV], total[:, DV:]

        position = iota((TOK, DV), 0) + i * TOK
        depth = position - jnp.where(iota((TOK, DV), 0) >= bound, opening(i), before)
        mixed = taps[0:1] * gates[pl.ds(8 + i * TOK, TOK)]
        for shift in range(1, CONV):
            moved = gates[pl.ds(8 - shift + i * TOK, TOK)]
            mixed += jnp.where(depth >= shift, taps[shift : shift + 1] * moved, 0.0)
        incoming = grad[i].astype(F32)
        gate = 1.0 / (1.0 + jnp.exp(-mixed))
        scale = 1.0 / den
        attended = num * scale
        d_num = incoming * mixed * gate * scale
        d_den = -jnp.sum(d_num * attended, axis=1, keepdims=True)
        mixed_grad = incoming * attended * gate * (1.0 + mixed * (1.0 - gate))
        mixed_grads[0, pl.ds(i * TOK, TOK)] = mixed_grad
        for shift in range(1, CONV):
            mixed_grads[shift, pl.ds(i * TOK, TOK)] = jnp.where(depth >= shift, mixed_grad, 0.0)

        d_pair = jnp.concatenate(halves(d_num), axis=1)
        d_pair_t = jnp.concatenate(halves(d_num.T), axis=0)

        def slopes(d_pair, d_den, base, value):
            return (nt(d_pair, jnp.concatenate([value, value], axis=1)) + d_den) * base

        slope = slopes(d_pair, d_den, own_base, values(i, 1))
        s_high, s_low = halves(jnp.where(same, slope, 0.0))
        key = keys(i, 1)
        lanes = pl.ds(i * TOK, TOK)
        dv_s[:, lanes] = nn(d_pair_t, own_high) + nn(d_pair_t, own_low)
        dk_s[:, lanes] = nn(query_t, s_high) + nn(query_t, s_low)
        dq_s[i] = nt(key, s_high) + nt(key, s_low)

        def backward(j, wide):
            width = wide * TOK
            lanes = pl.ds(j * TOK, width)
            lane_old = jnp.where(iota((2 * DV, TOK), 1) < bound, 1.0, 0.0).astype(BF16)
            row_old = jnp.where(old, 1.0, 0.0).astype(BF16)
            pair, pair_t = d_pair * row_old, d_pair_t * lane_old
            den = jnp.where(iota((TOK, 1), 0) < bound, d_den, 0.0)
            saved = pl.ds(room + j * TOK, width)
            s_high, s_low = halves(slopes(pair, den, base_s[:, saved], values(j, wide)))
            allowed = iota((1, width), 1) + j * TOK >= before
            keep = jnp.where(allowed, 1.0, 0.0)
            key = keys(j, wide) * keep.astype(BF16)
            dv_s[:, lanes] += keep * (nn(pair_t, high_s[:, saved]) + nn(pair_t, low_s[:, saved]))
            dk_s[:, lanes] += keep * (nn(query_t, s_high) + nn(query_t, s_low))
            dq_s[i] += nt(key, s_high) + nt(key, s_low)

        spans(i, backward)
        yield

    if count <= UNROLLED:
        rows = [row_block(i) for i in range(count)]
        for _ in range(2):
            for row in rows:
                next(row)
    else:
        each(0, count, lambda i: list(row_block(i)))

    for partner, out in zip(senders, outs):
        j = me ^ partner
        lanes = pl.ds(pl.multiple_of(j * TOK, TOK), TOK)
        total = dv_s[0:DV, lanes] + dv_s[DV : 2 * DV, lanes]
        out[0:TOK, 0:DV] = total.T.astype(BF16)
        back = taps[0:1] * mixed_grads[0, pl.ds(pl.multiple_of(j * TOK, TOK), TOK)]
        for shift in range(1, CONV):
            window = mixed_grads[shift, pl.ds(pl.multiple_of(j * TOK, TOK), TOK + 8)]
            back += taps[shift : shift + 1] * window[shift : shift + TOK]
        out[0:TOK, DV : 2 * DV] = back.astype(BF16)
        out[TOK : TOK + F] = (0.25 * dq_s[j]).astype(BF16)
        out[TOK + F : TOK + 2 * F] = dk_s[:, lanes].astype(BF16)


def attend(count, phase, bounds, taps, packed, grads):
    outs = len(senders_of(count))
    saved = (count * (count - 1) // 2 if count <= UNROLLED else count - 1) * TOK
    return pl.pallas_call(
        functools.partial(attend_kernel, count, phase),
        out_shape=[jax.ShapeDtypeStruct((ROWS, 2 * DV), BF16)] * outs,
        in_specs=[SMEM, VMEM] + [VMEM] * (len(packed) + len(grads)),
        out_specs=[VMEM] * outs,
        scratch_shapes=[
            pltpu.VMEM((count, ROWS, 2 * DV), BF16),
            pltpu.VMEM((count, TOK, DV), BF16),
            pltpu.VMEM((count * TOK + 8, DV), F32),
            pltpu.VMEM((CONV, count * TOK + 8, DV), F32),
            pltpu.VMEM((TOK, saved), BF16),
            pltpu.VMEM((TOK, saved), BF16),
            pltpu.VMEM((TOK, saved), F32),
            pltpu.VMEM((count, TOK, 2 * DV), F32),
            pltpu.VMEM((count, F, TOK), F32),
            pltpu.VMEM((F, count * TOK), F32),
            pltpu.VMEM((2 * DV, count * TOK), F32),
        ],
        compiler_params=params(count),
    )(bounds, taps, *packed, *grads)


def unpack_kernel(count, phase, *rest):
    senders = senders_of(count)
    many = len(senders)
    me = lax.axis_index("ctx")
    last = phase == phases_of(count) - 1
    arrived, rest = rest[:many], rest[many:]
    earlier = None
    if phase > 0:
        earlier, rest = rest[0], rest[3:]
    v_ref, gate_ref = rest[:2]
    sem = rest[-1]
    rows_ref = rest[-2] if last else rest[2]
    copies = []
    for n, partner in enumerate(senders):
        head = first_head(me ^ partner, count) + phase
        lanes = pl.ds(pl.multiple_of(head * DV, DV), DV)
        copies.append((arrived[n].at[0:TOK, 0:DV], v_ref.at[0, :, lanes]))
        copies.append((arrived[n].at[0:TOK, DV : 2 * DV], gate_ref.at[0, :, lanes]))
    copies = [pltpu.make_async_copy(a, b, sem.at[n]) for n, (a, b) in enumerate(copies)]
    for copy in copies:
        copy.start()
    if earlier is not None:
        rows_ref[...] = earlier[...]
    for n, partner in enumerate(senders):
        head = first_head(me ^ partner, count) + phase
        rows = pl.ds(pl.multiple_of(head * F, F), F)
        for side in range(2):
            rows_ref[side, rows] = arrived[n][TOK + side * F : TOK + (side + 1) * F]
    if last:
        for side, ref in enumerate(rest[2:4]):
            ref[0] = rows_ref[side].astype(F32).T.astype(BF16)
    for copy in copies:
        copy.wait()


def unpack(count, phase, arrived, begun):
    wide = jax.ShapeDtypeStruct((1, TOK, HEADS * DV), BF16)
    narrow = jax.ShapeDtypeStruct((1, TOK, HEADS * F), BF16)
    turned = (2, HEADS * F, TOK)
    last = phase == phases_of(count) - 1
    many = len(arrived)
    small = [narrow, narrow] if last else [jax.ShapeDtypeStruct(turned, BF16)]
    return pl.pallas_call(
        functools.partial(unpack_kernel, count, phase),
        out_shape=[wide, wide] + small,
        in_specs=[VMEM] * many + [VMEM, HBM, HBM][: len(begun)],
        out_specs=[HBM, HBM] + [VMEM] * len(small),
        input_output_aliases={many + 1: 0, many + 2: 1} if begun else {},
        scratch_shapes=([pltpu.VMEM(turned, BF16)] if last else [])
        + [pltpu.SemaphoreType.DMA((2 * many,))],
        compiler_params=params(count),
    )(*arrived, *begun)


def on_device(count, sections, q_in, k_in, v_in, gate_in, out_grad, conv_weight, bounds):
    phases, senders = phases_of(count), senders_of(count)

    def across(value, partner):
        if partner == 0:
            return value
        return lax.ppermute(value, "ctx", [(c, c ^ partner) for c in range(count)])

    def across_back(value, partner):
        pairs = [
            (c * sections + s, (c ^ partner) * sections + (s - 1) % sections)
            for c in range(count)
            for s in range(sections)
        ]
        return lax.ppermute(value, ("ctx", "pipe"), pairs)

    order = sorted(range(count), key=lambda partner: -bin(partner).count("1"))
    shift = [(s, (s - 1) % sections) for s in range(sections)]
    cotangent = lax.ppermute(out_grad, "pipe", shift)

    def spread(packed):
        moved = {partner: across(packed[partner], partner) for partner in order}
        return [moved[partner] for partner in range(count)]

    inputs = (q_in, k_in, v_in, gate_in)
    blocks = [spread(pack(count, 0, *inputs))]
    own_grads = pack_grads(count, cotangent)
    grads = spread(own_grads)
    for phase in range(1, phases):
        before = blocks[phase - 1][order[-2]], own_grads[0]
        blocks.append(spread(pack(count, phase, *inputs, cotangent, *before)))
    arrived = []
    for phase in range(phases):
        results = attend(count, phase, bounds, conv_weight, blocks[phase], grads)
        grads = []
        results = dict(zip(senders, results))
        moved = {p: across_back(results[p], p) for p in order if p in results}
        arrived.append([moved[partner] for partner in senders])
    begun = ()
    for phase in range(phases):
        out = unpack(count, phase, arrived[phase], begun)
        begun = (out[2], out[0], out[1])
    v_grad, gate_grad, q_grad, k_grad = out
    return q_grad, k_grad, v_grad, gate_grad


def solution(mesh):
    count, sections = mesh.shape["ctx"], mesh.shape["pipe"]
    split = P("pipe", "ctx", None)
    in_specs = (split,) * 5 + (P("pipe", None, None), P("pipe", None))
    return jax.shard_map(
        functools.partial(on_device, count, sections),
        mesh=mesh,
        in_specs=in_specs,
        out_specs=(split,) * 4,
        check_vma=False,
    )
```

```python
import functools

import jax
import jax.numpy as jnp
from jax import lax
from jax.experimental import pallas as pl
from jax.experimental.pallas import tpu as pltpu
from jax.sharding import PartitionSpec as P

HEADS = 8
F = 16
DV = 128
CONV = 3
TOK = 256
ROWS = TOK + 2 * F
BF16 = jnp.bfloat16
F32 = jnp.float32
UNROLLED = 4
HBM = pl.BlockSpec(memory_space=pltpu.HBM)

ANY = pl.BlockSpec(memory_space=pl.ANY)
SMEM = pl.BlockSpec(memory_space=pltpu.SMEM)
VMEM = pl.BlockSpec(memory_space=pltpu.VMEM)


def params(count):
    return pltpu.CompilerParams(vmem_limit_bytes=(14 if count <= UNROLLED else 44) * 1024 * 1024)


PACK_PARAMS = pltpu.CompilerParams(vmem_limit_bytes=125 * 512 * 1024)


def first_head(place, count):
    return (place * HEADS) // count


def cost(micros):
    return pl.CostEstimate(flops=int(1e9 * micros), bytes_accessed=int(3e6 * micros), transcendentals=0)


def lanes_of(head, width):
    return pl.ds(pl.multiple_of(head * width, width), width)


def phases_of(count):
    return max(1, HEADS // count)


def senders_of(count):
    return range(0, count, max(1, count // HEADS))


def pack_kernel(count, phase, q_ref, k_ref, v_ref, gate_ref, *rest):
    me = lax.axis_index("ctx")
    packed = rest[-4 - count : -4]
    rows, turned, sem, sem_rows = rest[-4:]
    copies = []
    for partner, out in enumerate(packed):
        lanes = lanes_of(first_head(me ^ partner, count) + phase, DV)
        copies.append((v_ref.at[0, :, lanes], out.at[0:TOK, 0:DV]))
        copies.append((gate_ref.at[0, :, lanes], out.at[0:TOK, DV : 2 * DV]))
    copies = [pltpu.make_async_copy(a, b, sem.at[n]) for n, (a, b) in enumerate(copies)]
    loads = [
        pltpu.make_async_copy(ref.at[0], rows.at[side], sem_rows.at[side])
        for side, ref in enumerate((q_ref, k_ref))
    ]
    for copy in loads + copies:
        copy.start()
    for side, copy in enumerate(loads):
        copy.wait()
        turned[side] = rows[side].astype(F32).T.astype(BF16)
    for partner, out in enumerate(packed):
        head = first_head(me ^ partner, count) + phase
        for side in range(2):
            mine = turned[side, lanes_of(head, F)]
            out[TOK + side * F : TOK + (side + 1) * F] = mine
    if phase > 0:
        grad_ref = rest[0]
        for partner, out in enumerate(packed):
            pack_grad(count, phase, me ^ partner, grad_ref, out)
    for copy in copies:
        copy.wait()


def pack_grad(count, phase, place, grad_ref, out):
    mine = grad_ref[0, :, lanes_of(first_head(place, count) + phase, DV)]
    half = TOK // 2
    base = 0 if phase == 0 else ROWS
    out[base : base + half, 0:DV] = mine[0:half]
    out[base : base + half, DV : 2 * DV] = mine[half:TOK]


def pack(count, phase, q_in, k_in, v_in, gate_in, *others):
    rows = ROWS if phase == 0 else ROWS + TOK // 2
    return pl.pallas_call(
        functools.partial(pack_kernel, count, phase),
        cost_estimate=cost(2),
        out_shape=[jax.ShapeDtypeStruct((rows, 2 * DV), BF16)] * count,
        in_specs=[HBM] * 4 + [VMEM] * min(1, len(others)) + [ANY] * max(0, len(others) - 1),
        out_specs=[VMEM] * count,
        scratch_shapes=[
            pltpu.VMEM((2, TOK, HEADS * F), BF16),
            pltpu.VMEM((2, HEADS * F, TOK), BF16),
            pltpu.SemaphoreType.DMA((2 * count,)),
            pltpu.SemaphoreType.DMA((2,)),
        ],
        compiler_params=PACK_PARAMS if phase == 0 else params(count),
    )(q_in, k_in, v_in, gate_in, *others)


def pack_grads_kernel(count, grad_ref, *outs):
    outs = outs[-count:]
    me = lax.axis_index("ctx")
    for partner, out in enumerate(outs):
        pack_grad(count, 0, me ^ partner, grad_ref, out)


def pack_grads(count, grad, *before):
    return pl.pallas_call(
        functools.partial(pack_grads_kernel, count),
        cost_estimate=cost(0.5),
        out_shape=[jax.ShapeDtypeStruct((TOK // 2, 2 * DV), BF16)] * count,
        in_specs=[VMEM] + [ANY] * len(before),
        out_specs=[VMEM] * count,
        compiler_params=params(count),
    )(grad, *before)


def nn(a, b):
    return lax.dot_general(a, b, (((1,), (0,)), ((), ())), preferred_element_type=F32)


def nt(a, b):
    return lax.dot_general(a, b, (((1,), (1,)), ((), ())), preferred_element_type=F32)


def halves(x):
    high = x.astype(BF16)
    return high, (x - high.astype(F32)).astype(BF16)


def iota(shape, dim):
    return lax.broadcasted_iota(jnp.int32, shape, dim)


def each(low, high, body):
    if isinstance(low, int) and isinstance(high, int) and high - low <= UNROLLED:
        for step in range(low, high):
            body(step)
    else:

        def one(step, carry):
            body(step)
            return carry

        lax.fori_loop(low, high, one, 0)


def attend_kernel(count, phase, bounds, taps_ref, *rest):
    senders = senders_of(count)
    packed, rest = rest[:count], rest[count:]
    grads, base = packed, ROWS
    if phase == 0:
        grads, base, rest = rest[:count], 0, rest[count:]
    outs = rest[: len(senders)]
    (block, grad, gates, mixed_grads, high_s, low_s, base_s, num_s, dq_s, dk_s, dv_s,
    ) = rest[len(senders) :]
    me = lax.axis_index("ctx")
    for partner in range(count):
        block[me ^ partner] = packed[partner][0:ROWS]
        for half in range(2):
            grad[me ^ partner, half * TOK // 2 : (half + 1) * TOK // 2] = grads[partner][
                base : base + TOK // 2, half * DV : (half + 1) * DV
            ]
    head = first_head(me, count) + phase
    taps = taps_ref[0, :, pl.ds(pl.multiple_of(head * DV, DV), DV)].astype(F32)
    gates[0:8] = jnp.zeros((8, DV), F32)
    mixed_grads[:, count * TOK : count * TOK + 8] = jnp.zeros((CONV, 8, DV), F32)

    def spread(j):
        gates[pl.ds(8 + j * TOK, TOK)] = block[j, 0:TOK, DV : 2 * DV].astype(F32)

    each(0, count, spread)

    def opening(i):
        bound = bounds[0, i]
        return jnp.where(bound < TOK, i * TOK + bound, 0)

    def earlier(i):
        if isinstance(i, int):
            last = jnp.int32(0)
            for j in range(i):
                last = jnp.maximum(last, opening(j))
            return last
        return lax.fori_loop(0, i, lambda j, last: jnp.maximum(last, opening(j)), jnp.int32(0))

    def values(j, wide):
        return block[pl.ds(j, wide), 0:TOK, 0:DV].reshape(wide * TOK, DV)

    def keys(j, wide):
        parts = [block[j + step, TOK + F : TOK + 2 * F] for step in range(wide)]
        return parts[0] if wide == 1 else jnp.concatenate(parts, axis=1)

    def spans(i, body):
        if isinstance(i, int):
            if i > 0:
                body(0, i)
        else:
            each(0, i, lambda j: body(j, 1))

    def row_block(i):
        bound = bounds[0, i]
        before = earlier(i)
        row, col = iota((TOK, TOK), 0), iota((TOK, TOK), 1)
        same = (col <= row) & ((col >= bound) | (row < bound))
        query_t = block[i, TOK : TOK + F] * BF16(0.25)
        query = query_t.astype(F32).T.astype(BF16)

        def kernel_of(j, wide):
            base = 1.0 + nn(query, keys(j, wide))
            return base, 0.5 * base * base + 0.5

        def weigh(high, low, value):
            value = jnp.concatenate([value, jnp.ones_like(value)], axis=1)
            return nn(high, value) + nn(low, value)

        own_base, own_kern = kernel_of(i, 1)
        own_high, own_low = halves(jnp.where(same, own_kern, 0.0))
        own = weigh(own_high, own_low, values(i, 1))
        num_s[i] = jnp.zeros((TOK, 2 * DV), F32)
        room = (i * (i - 1)) // 2 * TOK if isinstance(i, int) else 0

        def forward(j, wide):
            width = wide * TOK
            base, kern = kernel_of(j, wide)
            high, low = halves(kern)
            lanes = pl.ds(room + j * TOK, width)
            base_s[:, lanes] = base
            high_s[:, lanes] = high
            low_s[:, lanes] = low
            value = values(j, wide)
            allowed = iota((width, DV), 0) + j * TOK >= before
            ones = jnp.where(allowed, 1.0, 0.0).astype(BF16)
            value = jnp.concatenate([value * ones, ones], axis=1)
            num_s[i] += nn(high, value) + nn(low, value)

        spans(i, forward)
        yield
        old = iota((TOK, 2 * DV), 0) < bound
        total = own + jnp.where(old, num_s[i], 0.0)
        num, den = total[:, 0:DV], total[:, DV:]

        position = iota((TOK, DV), 0) + i * TOK
        depth = position - jnp.where(iota((TOK, DV), 0) >= bound, opening(i), before)
        mixed = taps[0:1] * gates[pl.ds(8 + i * TOK, TOK)]
        for shift in range(1, CONV):
            moved = gates[pl.ds(8 - shift + i * TOK, TOK)]
            mixed += jnp.where(depth >= shift, taps[shift : shift + 1] * moved, 0.0)
        incoming = grad[i].astype(F32)
        gate = 1.0 / (1.0 + jnp.exp(-mixed))
        scale = 1.0 / den
        attended = num * scale
        d_num = incoming * mixed * gate * scale
        d_den = -jnp.sum(d_num * attended, axis=1, keepdims=True)
        mixed_grad = incoming * attended * gate * (1.0 + mixed * (1.0 - gate))
        mixed_grads[0, pl.ds(i * TOK, TOK)] = mixed_grad
        for shift in range(1, CONV):
            mixed_grads[shift, pl.ds(i * TOK, TOK)] = jnp.where(depth >= shift, mixed_grad, 0.0)

        d_pair = jnp.concatenate(halves(d_num), axis=1)
        d_pair_t = jnp.concatenate(halves(d_num.T), axis=0)

        def slopes(d_pair, d_den, base, value):
            return (nt(d_pair, jnp.concatenate([value, value], axis=1)) + d_den) * base

        slope = slopes(d_pair, d_den, own_base, values(i, 1))
        s_high, s_low = halves(jnp.where(same, slope, 0.0))
        key = keys(i, 1)
        lanes = pl.ds(i * TOK, TOK)
        dv_s[:, lanes] = nn(d_pair_t, own_high) + nn(d_pair_t, own_low)
        dk_s[:, lanes] = nn(query_t, s_high) + nn(query_t, s_low)
        dq_s[i] = nt(key, s_high) + nt(key, s_low)

        def backward(j, wide):
            width = wide * TOK
            lanes = pl.ds(j * TOK, width)
            lane_old = jnp.where(iota((2 * DV, TOK), 1) < bound, 1.0, 0.0).astype(BF16)
            row_old = jnp.where(old, 1.0, 0.0).astype(BF16)
            pair, pair_t = d_pair * row_old, d_pair_t * lane_old
            den = jnp.where(iota((TOK, 1), 0) < bound, d_den, 0.0)
            saved = pl.ds(room + j * TOK, width)
            s_high, s_low = halves(slopes(pair, den, base_s[:, saved], values(j, wide)))
            allowed = iota((1, width), 1) + j * TOK >= before
            keep = jnp.where(allowed, 1.0, 0.0)
            key = keys(j, wide) * keep.astype(BF16)
            dv_s[:, lanes] += keep * (nn(pair_t, high_s[:, saved]) + nn(pair_t, low_s[:, saved]))
            dk_s[:, lanes] += keep * (nn(query_t, s_high) + nn(query_t, s_low))
            dq_s[i] += nt(key, s_high) + nt(key, s_low)

        spans(i, backward)
        yield

    if count <= UNROLLED:
        rows = [row_block(i) for i in range(count)]
        for _ in range(2):
            for row in rows:
                next(row)
    else:
        each(0, count, lambda i: list(row_block(i)))

    for partner, out in zip(senders, outs):
        j = me ^ partner
        lanes = pl.ds(pl.multiple_of(j * TOK, TOK), TOK)
        total = dv_s[0:DV, lanes] + dv_s[DV : 2 * DV, lanes]
        out[0:TOK, 0:DV] = total.T.astype(BF16)
        back = taps[0:1] * mixed_grads[0, pl.ds(pl.multiple_of(j * TOK, TOK), TOK)]
        for shift in range(1, CONV):
            window = mixed_grads[shift, pl.ds(pl.multiple_of(j * TOK, TOK), TOK + 8)]
            back += taps[shift : shift + 1] * window[shift : shift + TOK]
        out[0:TOK, DV : 2 * DV] = back.astype(BF16)
        out[TOK : TOK + F] = (0.25 * dq_s[j]).astype(BF16)
        out[TOK + F : TOK + 2 * F] = dk_s[:, lanes].astype(BF16)


def attend(count, phase, bounds, taps, packed, grads):
    outs = len(senders_of(count))
    saved = (count * (count - 1) // 2 if count <= UNROLLED else count - 1) * TOK
    return pl.pallas_call(
        functools.partial(attend_kernel, count, phase),
        cost_estimate=cost(5),
        out_shape=[jax.ShapeDtypeStruct((ROWS, 2 * DV), BF16)] * outs,
        in_specs=[SMEM, VMEM] + [VMEM] * (len(packed) + len(grads)),
        out_specs=[VMEM] * outs,
        scratch_shapes=[
            pltpu.VMEM((count, ROWS, 2 * DV), BF16),
            pltpu.VMEM((count, TOK, DV), BF16),
            pltpu.VMEM((count * TOK + 8, DV), F32),
            pltpu.VMEM((CONV, count * TOK + 8, DV), F32),
            pltpu.VMEM((TOK, saved), BF16),
            pltpu.VMEM((TOK, saved), BF16),
            pltpu.VMEM((TOK, saved), F32),
            pltpu.VMEM((count, TOK, 2 * DV), F32),
            pltpu.VMEM((count, F, TOK), F32),
            pltpu.VMEM((F, count * TOK), F32),
            pltpu.VMEM((2 * DV, count * TOK), F32),
        ],
        compiler_params=params(count),
    )(bounds, taps, *packed, *grads)


def unpack_kernel(count, phase, *rest):
    senders = senders_of(count)
    many = len(senders)
    me = lax.axis_index("ctx")
    last = phase == phases_of(count) - 1
    arrived, rest = rest[:many], rest[many:]
    earlier = None
    if phase > 0:
        earlier, rest = rest[0], rest[3:]
    v_ref, gate_ref = rest[:2]
    sem = rest[-1]
    rows_ref = rest[-2] if last else rest[2]
    copies = []
    for n, partner in enumerate(senders):
        head = first_head(me ^ partner, count) + phase
        lanes = pl.ds(pl.multiple_of(head * DV, DV), DV)
        copies.append((arrived[n].at[0:TOK, 0:DV], v_ref.at[0, :, lanes]))
        copies.append((arrived[n].at[0:TOK, DV : 2 * DV], gate_ref.at[0, :, lanes]))
    copies = [pltpu.make_async_copy(a, b, sem.at[n]) for n, (a, b) in enumerate(copies)]
    for copy in copies:
        copy.start()
    if earlier is not None:
        rows_ref[...] = earlier[...]
    for n, partner in enumerate(senders):
        head = first_head(me ^ partner, count) + phase
        rows = pl.ds(pl.multiple_of(head * F, F), F)
        for side in range(2):
            rows_ref[side, rows] = arrived[n][TOK + side * F : TOK + (side + 1) * F]
    if last:
        for side, ref in enumerate(rest[2:4]):
            ref[0] = rows_ref[side].astype(F32).T.astype(BF16)
    for copy in copies:
        copy.wait()


def unpack(count, phase, arrived, begun):
    wide = jax.ShapeDtypeStruct((1, TOK, HEADS * DV), BF16)
    narrow = jax.ShapeDtypeStruct((1, TOK, HEADS * F), BF16)
    turned = (2, HEADS * F, TOK)
    last = phase == phases_of(count) - 1
    many = len(arrived)
    small = [narrow, narrow] if last else [jax.ShapeDtypeStruct(turned, BF16)]
    return pl.pallas_call(
        functools.partial(unpack_kernel, count, phase),
        cost_estimate=cost(1),
        out_shape=[wide, wide] + small,
        in_specs=[VMEM] * many + [VMEM, HBM, HBM][: len(begun)],
        out_specs=[HBM, HBM] + [VMEM] * len(small),
        input_output_aliases={many + 1: 0, many + 2: 1} if begun else {},
        scratch_shapes=([pltpu.VMEM(turned, BF16)] if last else [])
        + [pltpu.SemaphoreType.DMA((2 * many,))],
        compiler_params=params(count),
    )(*arrived, *begun)


def on_device(count, sections, q_in, k_in, v_in, gate_in, out_grad, conv_weight, bounds):
    phases, senders = phases_of(count), senders_of(count)

    def across(value, partner):
        if partner == 0:
            return value
        return lax.ppermute(value, "ctx", [(c, c ^ partner) for c in range(count)])

    def across_back(value, partner):
        pairs = [
            (c * sections + s, (c ^ partner) * sections + (s - 1) % sections)
            for c in range(count)
            for s in range(sections)
        ]
        return lax.ppermute(value, ("ctx", "pipe"), pairs)

    order = sorted(range(count), key=lambda partner: -bin(partner).count("1"))
    shift = [(s, (s - 1) % sections) for s in range(sections)]
    cotangent = lax.ppermute(out_grad, "pipe", shift)

    def spread(packed):
        moved = {partner: across(packed[partner], partner) for partner in order}
        return [moved[partner] for partner in range(count)]

    inputs = (q_in, k_in, v_in, gate_in)
    blocks = [spread(pack(count, 0, *inputs))]
    own_grads = pack_grads(count, cotangent)
    grads = spread(own_grads)
    for phase in range(1, phases):
        before = [own_grads[0]]
        blocks.append(spread(pack(count, phase, *inputs, cotangent, *before)))
    arrived = []
    for phase in range(phases):
        results = attend(count, phase, bounds, conv_weight, blocks[phase], grads)
        grads = []
        results = dict(zip(senders, results))
        moved = {p: across_back(results[p], p) for p in order if p in results}
        arrived.append([moved[partner] for partner in senders])
    begun = ()
    for phase in range(phases):
        out = unpack(count, phase, arrived[phase], begun)
        begun = (out[2], out[0], out[1])
    v_grad, gate_grad, q_grad, k_grad = out
    return q_grad, k_grad, v_grad, gate_grad


def solution(mesh):
    count, sections = mesh.shape["ctx"], mesh.shape["pipe"]
    split = P("pipe", "ctx", None)
    in_specs = (split,) * 5 + (P("pipe", None, None), P("pipe", None))
    return jax.shard_map(
        functools.partial(on_device, count, sections),
        mesh=mesh,
        in_specs=in_specs,
        out_specs=(split,) * 4,
        check_vma=False,
    )
```

```python
import functools

import jax
import jax.numpy as jnp
from jax import lax
from jax.experimental import pallas as pl
from jax.experimental.pallas import tpu as pltpu
from jax.sharding import PartitionSpec as P

HEADS = 8
F = 16
DV = 128
CONV = 3
TOK = 256
ROWS = TOK + 2 * F
BF16 = jnp.bfloat16
F32 = jnp.float32
UNROLLED = 4
HBM = pl.BlockSpec(memory_space=pltpu.HBM)

ANY = pl.BlockSpec(memory_space=pl.ANY)
SMEM = pl.BlockSpec(memory_space=pltpu.SMEM)
VMEM = pl.BlockSpec(memory_space=pltpu.VMEM)


def params(count):
    return pltpu.CompilerParams(vmem_limit_bytes=(14 if count <= UNROLLED else 44) * 1024 * 1024)


PACK_PARAMS = pltpu.CompilerParams(vmem_limit_bytes=125 * 512 * 1024)


def first_head(place, count):
    return (place * HEADS) // count


def cost(micros):
    return pl.CostEstimate(flops=int(1e9 * micros), bytes_accessed=int(3e6 * micros), transcendentals=0)


def lanes_of(head, width):
    return pl.ds(pl.multiple_of(head * width, width), width)


def phases_of(count):
    return max(1, HEADS // count)


def senders_of(count):
    return [p for p in (sorted(range(count), key=lambda p: -bin(p).count('1'))) if p % max(1, count // HEADS) == 0]


def pack_kernel(count, phase, q_ref, k_ref, v_ref, gate_ref, *rest):
    me = lax.axis_index("ctx")
    packed = rest[-4 - count : -4]
    rows, turned, sem, sem_rows = rest[-4:]
    copies = []
    for partner, out in enumerate(packed):
        lanes = lanes_of(first_head(me ^ partner, count) + phase, DV)
        copies.append((v_ref.at[0, :, lanes], out.at[0:TOK, 0:DV]))
        copies.append((gate_ref.at[0, :, lanes], out.at[0:TOK, DV : 2 * DV]))
    copies = [pltpu.make_async_copy(a, b, sem.at[n]) for n, (a, b) in enumerate(copies)]
    loads = [
        pltpu.make_async_copy(ref.at[0], rows.at[side], sem_rows.at[side])
        for side, ref in enumerate((q_ref, k_ref))
    ]
    for copy in loads + copies:
        copy.start()
    for side, copy in enumerate(loads):
        copy.wait()
        turned[side] = rows[side].astype(F32).T.astype(BF16)
    for partner, out in enumerate(packed):
        head = first_head(me ^ partner, count) + phase
        for side in range(2):
            mine = turned[side, lanes_of(head, F)]
            out[TOK + side * F : TOK + (side + 1) * F] = mine
    if phase > 0:
        grad_ref = rest[0]
        for partner, out in enumerate(packed):
            pack_grad(count, phase, me ^ partner, grad_ref, out)
    for copy in copies:
        copy.wait()


def pack_grad(count, phase, place, grad_ref, out):
    mine = grad_ref[0, :, lanes_of(first_head(place, count) + phase, DV)]
    half = TOK // 2
    base = 0 if phase == 0 else ROWS
    out[base : base + half, 0:DV] = mine[0:half]
    out[base : base + half, DV : 2 * DV] = mine[half:TOK]


def pack(count, phase, q_in, k_in, v_in, gate_in, *others):
    rows = ROWS if phase == 0 else ROWS + TOK // 2
    return pl.pallas_call(
        functools.partial(pack_kernel, count, phase),
        cost_estimate=cost(2),
        out_shape=[jax.ShapeDtypeStruct((rows, 2 * DV), BF16)] * count,
        in_specs=[HBM] * 4 + [VMEM] * min(1, len(others)) + [ANY] * max(0, len(others) - 1),
        out_specs=[VMEM] * count,
        scratch_shapes=[
            pltpu.VMEM((2, TOK, HEADS * F), BF16),
            pltpu.VMEM((2, HEADS * F, TOK), BF16),
            pltpu.SemaphoreType.DMA((2 * count,)),
            pltpu.SemaphoreType.DMA((2,)),
        ],
        compiler_params=PACK_PARAMS if phase == 0 else params(count),
    )(q_in, k_in, v_in, gate_in, *others)


def pack_grads_kernel(count, grad_ref, *outs):
    outs = outs[-count:]
    me = lax.axis_index("ctx")
    for partner, out in enumerate(outs):
        pack_grad(count, 0, me ^ partner, grad_ref, out)


def pack_grads(count, grad, *before):
    return pl.pallas_call(
        functools.partial(pack_grads_kernel, count),
        cost_estimate=cost(0.5),
        out_shape=[jax.ShapeDtypeStruct((TOK // 2, 2 * DV), BF16)] * count,
        in_specs=[VMEM] + [ANY] * len(before),
        out_specs=[VMEM] * count,
        compiler_params=params(count),
    )(grad, *before)


def nn(a, b):
    return lax.dot_general(a, b, (((1,), (0,)), ((), ())), preferred_element_type=F32)


def nt(a, b):
    return lax.dot_general(a, b, (((1,), (1,)), ((), ())), preferred_element_type=F32)


def halves(x):
    high = x.astype(BF16)
    return high, (x - high.astype(F32)).astype(BF16)


def iota(shape, dim):
    return lax.broadcasted_iota(jnp.int32, shape, dim)


def each(low, high, body):
    if isinstance(low, int) and isinstance(high, int) and high - low <= UNROLLED:
        for step in range(low, high):
            body(step)
    else:

        def one(step, carry):
            body(step)
            return carry

        lax.fori_loop(low, high, one, 0)


def attend_kernel(count, phase, bounds, taps_ref, *rest):
    senders = senders_of(count)
    packed, rest = dict(zip((sorted(range(count), key=lambda p: -bin(p).count('1'))), rest)), rest[count:]
    grads, base = packed, ROWS
    if phase == 0:
        grads, base, rest = dict(zip((sorted(range(count), key=lambda p: -bin(p).count('1'))), rest)), 0, rest[count:]
    outs = rest[: len(senders)]
    (block, grad, gates, mixed_grads, high_s, low_s, base_s, num_s, dq_s, dk_s, dv_s,
    ) = rest[len(senders) :]
    me = lax.axis_index("ctx")
    for partner in range(count):
        block[me ^ partner] = packed[partner][0:ROWS]
        for half in range(2):
            grad[me ^ partner, half * TOK // 2 : (half + 1) * TOK // 2] = grads[partner][
                base : base + TOK // 2, half * DV : (half + 1) * DV
            ]
    head = first_head(me, count) + phase
    taps = taps_ref[0, :, pl.ds(pl.multiple_of(head * DV, DV), DV)].astype(F32)
    gates[0:8] = jnp.zeros((8, DV), F32)
    mixed_grads[:, count * TOK : count * TOK + 8] = jnp.zeros((CONV, 8, DV), F32)

    def spread(j):
        gates[pl.ds(8 + j * TOK, TOK)] = block[j, 0:TOK, DV : 2 * DV].astype(F32)

    each(0, count, spread)

    def opening(i):
        bound = bounds[0, i]
        return jnp.where(bound < TOK, i * TOK + bound, 0)

    def earlier(i):
        if isinstance(i, int):
            last = jnp.int32(0)
            for j in range(i):
                last = jnp.maximum(last, opening(j))
            return last
        return lax.fori_loop(0, i, lambda j, last: jnp.maximum(last, opening(j)), jnp.int32(0))

    def values(j, wide):
        return block[pl.ds(j, wide), 0:TOK, 0:DV].reshape(wide * TOK, DV)

    def keys(j, wide):
        parts = [block[j + step, TOK + F : TOK + 2 * F] for step in range(wide)]
        return parts[0] if wide == 1 else jnp.concatenate(parts, axis=1)

    def spans(i, body):
        if isinstance(i, int):
            for j in range(i):
                body(j, 1)
        else:
            each(0, i, lambda j: body(j, 1))

    def row_block(i):
        bound = bounds[0, i]
        before = earlier(i)
        row, col = iota((TOK, TOK), 0), iota((TOK, TOK), 1)
        same = (col <= row) & ((col >= bound) | (row < bound))
        query_t = block[i, TOK : TOK + F] * BF16(0.25)
        query = query_t.astype(F32).T.astype(BF16)
        query_t = query_t * BF16(2)

        def kernel_of(j, wide):
            base = 1.0 + nn(query, keys(j, wide))
            return base, base * base + 1.0

        def weigh(high, low, value):
            value = jnp.concatenate([value, jnp.ones_like(value)], axis=1)
            return nn(high, value) + nn(low, value)

        own_base, own_kern = kernel_of(i, 1)
        own_high, own_low = halves(jnp.where(same, own_kern, 0.0))
        own = weigh(own_high, own_low, values(i, 1))
        num_s[i] = jnp.zeros((TOK, 2 * DV), F32)
        room = (i * (i - 1)) // 2 * TOK if isinstance(i, int) else 0

        def forward(j, wide):
            width = wide * TOK
            base, kern = kernel_of(j, wide)
            high, low = halves(kern)
            lanes = pl.ds(room + j * TOK, width)
            base_s[:, lanes] = base
            high_s[:, lanes] = high
            low_s[:, lanes] = low
            value = values(j, wide)
            allowed = iota((width, DV), 0) + j * TOK >= before
            ones = jnp.where(allowed, 1.0, 0.0).astype(BF16)
            value = jnp.concatenate([value * ones, ones], axis=1)
            num_s[i] += nn(high, value) + nn(low, value)

        spans(i, forward)
        yield
        old = iota((TOK, 2 * DV), 0) < bound
        total = own + jnp.where(old, num_s[i], 0.0)
        num, den = total[:, 0:DV], total[:, DV:]

        position = iota((TOK, DV), 0) + i * TOK
        depth = position - jnp.where(iota((TOK, DV), 0) >= bound, opening(i), before)
        mixed = taps[0:1] * gates[pl.ds(8 + i * TOK, TOK)]
        for shift in range(1, CONV):
            moved = gates[pl.ds(8 - shift + i * TOK, TOK)]
            mixed += jnp.where(depth >= shift, taps[shift : shift + 1] * moved, 0.0)
        incoming = grad[i].astype(F32)
        gate = 1.0 / (1.0 + jnp.exp(-mixed))
        scale = 1.0 / den
        attended = num * scale
        d_num = incoming * mixed * gate * scale
        d_den = -jnp.sum(d_num * attended, axis=1, keepdims=True)
        mixed_grad = incoming * attended * gate * (1.0 + mixed * (1.0 - gate))
        mixed_grads[0, pl.ds(i * TOK, TOK)] = mixed_grad
        for shift in range(1, CONV):
            mixed_grads[shift, pl.ds(i * TOK, TOK)] = jnp.where(depth >= shift, mixed_grad, 0.0)

        d_pair = jnp.concatenate(halves(d_num), axis=1)
        d_pair_t = jnp.concatenate(halves(d_num.T), axis=0)

        def slopes(d_pair, d_den, base, value):
            return (nt(d_pair, jnp.concatenate([value, value], axis=1)) + d_den) * base

        slope = slopes(d_pair, d_den, own_base, values(i, 1))
        s_high, s_low = halves(jnp.where(same, slope, 0.0))
        key = keys(i, 1)
        lanes = pl.ds(i * TOK, TOK)
        dv_s[:, lanes] = nn(d_pair_t, own_high) + nn(d_pair_t, own_low)
        dk_s[:, lanes] = nn(query_t, s_high) + nn(query_t, s_low)
        dq_s[i] = nt(key, s_high) + nt(key, s_low)

        def backward(j, wide):
            width = wide * TOK
            lanes = pl.ds(j * TOK, width)
            lane_old = jnp.where(iota((2 * DV, TOK), 1) < bound, 1.0, 0.0).astype(BF16)
            row_old = jnp.where(old, 1.0, 0.0).astype(BF16)
            pair, pair_t = d_pair * row_old, d_pair_t * lane_old
            den = jnp.where(iota((TOK, 1), 0) < bound, d_den, 0.0)
            saved = pl.ds(room + j * TOK, width)
            s_high, s_low = halves(slopes(pair, den, base_s[:, saved], values(j, wide)))
            allowed = iota((1, width), 1) + j * TOK >= before
            keep = jnp.where(allowed, 1.0, 0.0)
            key = keys(j, wide) * keep.astype(BF16)
            dv_s[:, lanes] += keep * (nn(pair_t, high_s[:, saved]) + nn(pair_t, low_s[:, saved]))
            dk_s[:, lanes] += keep * (nn(query_t, s_high) + nn(query_t, s_low))
            dq_s[i] += nt(key, s_high) + nt(key, s_low)

        spans(i, backward)
        yield

    if count <= UNROLLED:
        rows = [row_block(i) for i in range(count)]
        for _ in range(2):
            for row in rows:
                next(row)
    else:
        each(0, count, lambda i: list(row_block(i)))

    for partner, out in zip(senders, outs):
        j = me ^ partner
        lanes = pl.ds(pl.multiple_of(j * TOK, TOK), TOK)
        total = dv_s[0:DV, lanes] + dv_s[DV : 2 * DV, lanes]
        out[0:TOK, 0:DV] = total.T.astype(BF16)
        back = taps[0:1] * mixed_grads[0, pl.ds(pl.multiple_of(j * TOK, TOK), TOK)]
        for shift in range(1, CONV):
            window = mixed_grads[shift, pl.ds(pl.multiple_of(j * TOK, TOK), TOK + 8)]
            back += taps[shift : shift + 1] * window[shift : shift + TOK]
        out[0:TOK, DV : 2 * DV] = back.astype(BF16)
        out[TOK : TOK + F] = (0.5 * dq_s[j]).astype(BF16)
        out[TOK + F : TOK + 2 * F] = dk_s[:, lanes].astype(BF16)


def attend(count, phase, bounds, taps, packed, grads):
    outs = len(senders_of(count))
    saved = (count * (count - 1) // 2 if count <= UNROLLED else count - 1) * TOK
    return pl.pallas_call(
        functools.partial(attend_kernel, count, phase),
        cost_estimate=cost(5),
        out_shape=[jax.ShapeDtypeStruct((ROWS, 2 * DV), BF16)] * outs,
        in_specs=[SMEM, VMEM] + [VMEM] * (len(packed) + len(grads)),
        out_specs=[VMEM] * outs,
        scratch_shapes=[
            pltpu.VMEM((count, ROWS, 2 * DV), BF16),
            pltpu.VMEM((count, TOK, DV), BF16),
            pltpu.VMEM((count * TOK + 8, DV), F32),
            pltpu.VMEM((CONV, count * TOK + 8, DV), F32),
            pltpu.VMEM((TOK, saved), BF16),
            pltpu.VMEM((TOK, saved), BF16),
            pltpu.VMEM((TOK, saved), F32),
            pltpu.VMEM((count, TOK, 2 * DV), F32),
            pltpu.VMEM((count, F, TOK), F32),
            pltpu.VMEM((F, count * TOK), F32),
            pltpu.VMEM((2 * DV, count * TOK), F32),
        ],
        compiler_params=params(count),
    )(bounds, taps, *[packed[p] for p in (sorted(range(count), key=lambda p: -bin(p).count('1')))], *[grads[p] for p in (sorted(range(count), key=lambda p: -bin(p).count('1'))) if grads])


def unpack_kernel(count, phase, *rest):
    senders = senders_of(count)
    many = len(senders)
    me = lax.axis_index("ctx")
    last = phase == phases_of(count) - 1
    arrived, rest = rest[:many], rest[many:]
    earlier = None
    if phase > 0:
        earlier, rest = rest[0], rest[3:]
    v_ref, gate_ref = rest[:2]
    sem = rest[-1]
    rows_ref = rest[-2] if last else rest[2]
    copies = []
    for n, partner in enumerate(senders):
        head = first_head(me ^ partner, count) + phase
        lanes = pl.ds(pl.multiple_of(head * DV, DV), DV)
        copies.append((arrived[n].at[0:TOK, 0:DV], v_ref.at[0, :, lanes]))
        copies.append((arrived[n].at[0:TOK, DV : 2 * DV], gate_ref.at[0, :, lanes]))
    copies = [pltpu.make_async_copy(a, b, sem.at[n]) for n, (a, b) in enumerate(copies)]
    for copy in copies:
        copy.start()
    if earlier is not None:
        rows_ref[...] = earlier[...]
    for n, partner in enumerate(senders):
        head = first_head(me ^ partner, count) + phase
        rows = pl.ds(pl.multiple_of(head * F, F), F)
        for side in range(2):
            rows_ref[side, rows] = arrived[n][TOK + side * F : TOK + (side + 1) * F]
    if last:
        for side, ref in enumerate(rest[2:4]):
            ref[0] = rows_ref[side].astype(F32).T.astype(BF16)
    for copy in copies:
        copy.wait()


def unpack(count, phase, arrived, begun):
    wide = jax.ShapeDtypeStruct((1, TOK, HEADS * DV), BF16)
    narrow = jax.ShapeDtypeStruct((1, TOK, HEADS * F), BF16)
    turned = (2, HEADS * F, TOK)
    last = phase == phases_of(count) - 1
    many = len(arrived)
    small = [narrow, narrow] if last else [jax.ShapeDtypeStruct(turned, BF16)]
    return pl.pallas_call(
        functools.partial(unpack_kernel, count, phase),
        cost_estimate=cost(1),
        out_shape=[wide, wide] + small,
        in_specs=[VMEM] * many + [VMEM, HBM, HBM][: len(begun)],
        out_specs=[HBM, HBM] + [VMEM] * len(small),
        input_output_aliases={many + 1: 0, many + 2: 1} if begun else {},
        scratch_shapes=([pltpu.VMEM(turned, BF16)] if last else [])
        + [pltpu.SemaphoreType.DMA((2 * many,))],
        compiler_params=params(count),
    )(*arrived, *begun)


def on_device(count, sections, q_in, k_in, v_in, gate_in, out_grad, conv_weight, bounds):
    phases, senders = phases_of(count), senders_of(count)

    def across(value, partner):
        if partner == 0:
            return value
        return lax.ppermute(value, "ctx", [(c, c ^ partner) for c in range(count)])

    def across_back(value, partner):
        pairs = [
            (c * sections + s, (c ^ partner) * sections + (s - 1) % sections)
            for c in range(count)
            for s in range(sections)
        ]
        return lax.ppermute(value, ("ctx", "pipe"), pairs)

    order = sorted(range(count), key=lambda partner: -bin(partner).count("1"))
    shift = [(s, (s - 1) % sections) for s in range(sections)]
    cotangent = lax.ppermute(out_grad, "pipe", shift)

    def spread(packed):
        moved = {partner: across(packed[partner], partner) for partner in order}
        return [moved[partner] for partner in range(count)]

    inputs = (q_in, k_in, v_in, gate_in)
    blocks = [spread(pack(count, 0, *inputs))]
    own_grads = pack_grads(count, cotangent)
    grads = spread(own_grads)
    for phase in range(1, phases):
        before = [own_grads[0]]
        blocks.append(spread(pack(count, phase, *inputs, cotangent, *before)))
    arrived = []
    for phase in range(phases):
        results = attend(count, phase, bounds, conv_weight, blocks[phase], grads)
        grads = []
        results = dict(zip(senders, results))
        moved = {p: across_back(results[p], p) for p in order if p in results}
        arrived.append([moved[partner] for partner in senders])
    begun = ()
    for phase in range(phases):
        out = unpack(count, phase, arrived[phase], begun)
        begun = (out[2], out[0], out[1])
    v_grad, gate_grad, q_grad, k_grad = out
    return q_grad, k_grad, v_grad, gate_grad


def solution(mesh):
    count, sections = mesh.shape["ctx"], mesh.shape["pipe"]
    split = P("pipe", "ctx", None)
    in_specs = (split,) * 5 + (P("pipe", None, None), P("pipe", None))
    return jax.shard_map(
        functools.partial(on_device, count, sections),
        mesh=mesh,
        in_specs=in_specs,
        out_specs=(split,) * 4,
        check_vma=False,
    )
```

```python
import functools

import jax
import jax.numpy as jnp
from jax import lax
from jax.experimental import pallas as pl
from jax.experimental.pallas import tpu as pltpu
from jax.sharding import PartitionSpec as P

HEADS = 8
F = 16
DV = 128
CONV = 3
TOK = 256
ROWS = TOK + 2 * F
BF16 = jnp.bfloat16
F32 = jnp.float32
UNROLLED = 4
HBM = pl.BlockSpec(memory_space=pltpu.HBM)

ANY = pl.BlockSpec(memory_space=pl.ANY)
SMEM = pl.BlockSpec(memory_space=pltpu.SMEM)
VMEM = pl.BlockSpec(memory_space=pltpu.VMEM)


def params(count):
    return pltpu.CompilerParams(vmem_limit_bytes=(14 if count <= UNROLLED else 44) * 1024 * 1024)


PACK_PARAMS = pltpu.CompilerParams(vmem_limit_bytes=125 * 512 * 1024)


def first_head(place, count):
    return (place * HEADS) // count


def cost(micros):
    return pl.CostEstimate(flops=int(1e9 * micros), bytes_accessed=int(3e6 * micros), transcendentals=0)


def lanes_of(head, width):
    return pl.ds(pl.multiple_of(head * width, width), width)


def phases_of(count):
    return max(1, HEADS // count)


def far_first(count):
    return sorted(range(count), key=lambda partner: -bin(partner).count("1"))


def senders_of(count):
    return [p for p in far_first(count) if p % max(1, count // HEADS) == 0]


def pack_kernel(count, phase, q_ref, k_ref, v_ref, gate_ref, *rest):
    me = lax.axis_index("ctx")
    packed = rest[-4 - count : -4]
    rows, turned, sem, sem_rows = rest[-4:]
    copies = []
    for partner, out in enumerate(packed):
        lanes = lanes_of(first_head(me ^ partner, count) + phase, DV)
        copies.append((v_ref.at[0, :, lanes], out.at[0:TOK, 0:DV]))
        copies.append((gate_ref.at[0, :, lanes], out.at[0:TOK, DV : 2 * DV]))
    copies = [pltpu.make_async_copy(a, b, sem.at[n]) for n, (a, b) in enumerate(copies)]
    loads = [
        pltpu.make_async_copy(ref.at[0], rows.at[side], sem_rows.at[side])
        for side, ref in enumerate((q_ref, k_ref))
    ]
    for copy in loads + copies:
        copy.start()
    for side, copy in enumerate(loads):
        copy.wait()
        turned[side] = rows[side].astype(F32).T.astype(BF16)
    for partner, out in enumerate(packed):
        head = first_head(me ^ partner, count) + phase
        for side in range(2):
            mine = turned[side, lanes_of(head, F)]
            out[TOK + side * F : TOK + (side + 1) * F] = mine
    if phase > 0:
        grad_ref = rest[0]
        for partner, out in enumerate(packed):
            pack_grad(count, phase, me ^ partner, grad_ref, out)
    for copy in copies:
        copy.wait()


def pack_grad(count, phase, place, grad_ref, out):
    mine = grad_ref[0, :, lanes_of(first_head(place, count) + phase, DV)]
    half = TOK // 2
    base = 0 if phase == 0 else ROWS
    out[base : base + half, 0:DV] = mine[0:half]
    out[base : base + half, DV : 2 * DV] = mine[half:TOK]


def pack(count, phase, q_in, k_in, v_in, gate_in, *others):
    rows = ROWS if phase == 0 else ROWS + TOK // 2
    return pl.pallas_call(
        functools.partial(pack_kernel, count, phase),
        cost_estimate=cost(2),
        out_shape=[jax.ShapeDtypeStruct((rows, 2 * DV), BF16)] * count,
        in_specs=[HBM] * 4 + [VMEM] * min(1, len(others)) + [ANY] * max(0, len(others) - 1),
        out_specs=[VMEM] * count,
        scratch_shapes=[
            pltpu.VMEM((2, TOK, HEADS * F), BF16),
            pltpu.VMEM((2, HEADS * F, TOK), BF16),
            pltpu.SemaphoreType.DMA((2 * count,)),
            pltpu.SemaphoreType.DMA((2,)),
        ],
        compiler_params=PACK_PARAMS if phase == 0 else params(count),
    )(q_in, k_in, v_in, gate_in, *others)


def pack_grads_kernel(count, grad_ref, *outs):
    outs = outs[-count:]
    me = lax.axis_index("ctx")
    for partner, out in enumerate(outs):
        pack_grad(count, 0, me ^ partner, grad_ref, out)


def pack_grads(count, grad, *before):
    return pl.pallas_call(
        functools.partial(pack_grads_kernel, count),
        cost_estimate=cost(0.5),
        out_shape=[jax.ShapeDtypeStruct((TOK // 2, 2 * DV), BF16)] * count,
        in_specs=[VMEM] + [ANY] * len(before),
        out_specs=[VMEM] * count,
        compiler_params=params(count),
    )(grad, *before)


def nn(a, b):
    return lax.dot_general(a, b, (((1,), (0,)), ((), ())), preferred_element_type=F32)


def nt(a, b):
    return lax.dot_general(a, b, (((1,), (1,)), ((), ())), preferred_element_type=F32)


def halves(x):
    high = x.astype(BF16)
    return high, (x - high.astype(F32)).astype(BF16)


def iota(shape, dim):
    return lax.broadcasted_iota(jnp.int32, shape, dim)


def each(low, high, body):
    if isinstance(low, int) and isinstance(high, int) and high - low <= UNROLLED:
        for step in range(low, high):
            body(step)
    else:

        def one(step, carry):
            body(step)
            return carry

        lax.fori_loop(low, high, one, 0)


def attend_kernel(count, phase, bounds, taps_ref, *rest):
    senders = senders_of(count)
    packed, rest = dict(zip(far_first(count), rest)), rest[count:]
    grads, base = packed, ROWS
    if phase == 0:
        grads, base, rest = dict(zip(far_first(count), rest)), 0, rest[count:]
    outs = rest[: len(senders)]
    (block, grad, gates, mixed_grads, high_s, low_s, base_s, num_s, dq_s, dk_s, dv_s,
    ) = rest[len(senders) :]
    me = lax.axis_index("ctx")
    for partner in range(count):
        block[me ^ partner] = packed[partner][0:ROWS]
        for half in range(2):
            grad[me ^ partner, half * TOK // 2 : (half + 1) * TOK // 2] = grads[partner][
                base : base + TOK // 2, half * DV : (half + 1) * DV
            ]
    head = first_head(me, count) + phase
    taps = taps_ref[0, :, pl.ds(pl.multiple_of(head * DV, DV), DV)].astype(F32)
    gates[0:8] = jnp.zeros((8, DV), F32)
    mixed_grads[:, count * TOK : count * TOK + 8] = jnp.zeros((CONV, 8, DV), F32)

    def spread(j):
        gates[pl.ds(8 + j * TOK, TOK)] = block[j, 0:TOK, DV : 2 * DV].astype(F32)

    each(0, count, spread)

    def opening(i):
        bound = bounds[0, i]
        return jnp.where(bound < TOK, i * TOK + bound, 0)

    def earlier(i):
        if isinstance(i, int):
            last = jnp.int32(0)
            for j in range(i):
                last = jnp.maximum(last, opening(j))
            return last
        return lax.fori_loop(0, i, lambda j, last: jnp.maximum(last, opening(j)), jnp.int32(0))

    def values(j, wide):
        return block[pl.ds(j, wide), 0:TOK, 0:DV].reshape(wide * TOK, DV)

    def keys(j, wide):
        parts = [block[j + step, TOK + F : TOK + 2 * F] for step in range(wide)]
        return parts[0] if wide == 1 else jnp.concatenate(parts, axis=1)

    def spans(i, body):
        if isinstance(i, int):
            for j in range(i):
                body(j, 1)
        else:
            each(0, i, lambda j: body(j, 1))

    def row_block(i):
        bound = bounds[0, i]
        before = earlier(i)
        row, col = iota((TOK, TOK), 0), iota((TOK, TOK), 1)
        same = (col <= row) & ((col >= bound) | (row < bound))
        query_t = block[i, TOK : TOK + F] * BF16(0.25)
        query = query_t.astype(F32).T.astype(BF16)
        query_t = query_t * BF16(2)

        def kernel_of(j, wide):
            base = 1.0 + nn(query, keys(j, wide))
            return base, base * base + 1.0

        def weigh(high, low, value):
            value = jnp.concatenate([value, jnp.ones_like(value)], axis=1)
            return nn(high, value) + nn(low, value)

        own_base, own_kern = kernel_of(i, 1)
        own_high, own_low = halves(jnp.where(same, own_kern, 0.0))
        own = weigh(own_high, own_low, values(i, 1))
        num_s[i] = jnp.zeros((TOK, 2 * DV), F32)
        room = (i * (i - 1)) // 2 * TOK if isinstance(i, int) else 0

        def forward(j, wide):
            width = wide * TOK
            base, kern = kernel_of(j, wide)
            high, low = halves(kern)
            lanes = pl.ds(room + j * TOK, width)
            base_s[:, lanes] = base
            high_s[:, lanes] = high
            low_s[:, lanes] = low
            value = values(j, wide)
            allowed = iota((width, DV), 0) + j * TOK >= before
            ones = jnp.where(allowed, 1.0, 0.0).astype(BF16)
            value = jnp.concatenate([value * ones, ones], axis=1)
            num_s[i] += nn(high, value) + nn(low, value)

        spans(i, forward)
        yield
        old = iota((TOK, 2 * DV), 0) < bound
        total = own + jnp.where(old, num_s[i], 0.0)
        num, den = total[:, 0:DV], total[:, DV:]

        position = iota((TOK, DV), 0) + i * TOK
        depth = position - jnp.where(iota((TOK, DV), 0) >= bound, opening(i), before)
        mixed = taps[0:1] * gates[pl.ds(8 + i * TOK, TOK)]
        for shift in range(1, CONV):
            moved = gates[pl.ds(8 - shift + i * TOK, TOK)]
            mixed += jnp.where(depth >= shift, taps[shift : shift + 1] * moved, 0.0)
        incoming = grad[i].astype(F32)
        gate = 1.0 / (1.0 + jnp.exp(-mixed))
        scale = 1.0 / den
        attended = num * scale
        d_num = incoming * mixed * gate * scale
        d_den = -jnp.sum(d_num * attended, axis=1, keepdims=True)
        mixed_grad = incoming * attended * gate * (1.0 + mixed * (1.0 - gate))
        mixed_grads[0, pl.ds(i * TOK, TOK)] = mixed_grad
        for shift in range(1, CONV):
            mixed_grads[shift, pl.ds(i * TOK, TOK)] = jnp.where(depth >= shift, mixed_grad, 0.0)

        d_pair = jnp.concatenate(halves(d_num), axis=1)
        d_pair_t = jnp.concatenate(halves(d_num.T), axis=0)

        def slopes(d_pair, d_den, base, value):
            return (nt(d_pair, jnp.concatenate([value, value], axis=1)) + d_den) * base

        slope = slopes(d_pair, d_den, own_base, values(i, 1))
        s_high, s_low = halves(jnp.where(same, slope, 0.0))
        key = keys(i, 1)
        lanes = pl.ds(i * TOK, TOK)
        dv_s[:, lanes] = nn(d_pair_t, own_high) + nn(d_pair_t, own_low)
        dk_s[:, lanes] = nn(query_t, s_high) + nn(query_t, s_low)
        dq_s[i] = nt(key, s_high) + nt(key, s_low)

        def backward(j, wide):
            width = wide * TOK
            lanes = pl.ds(j * TOK, width)
            lane_old = jnp.where(iota((2 * DV, TOK), 1) < bound, 1.0, 0.0).astype(BF16)
            row_old = jnp.where(old, 1.0, 0.0).astype(BF16)
            pair, pair_t = d_pair * row_old, d_pair_t * lane_old
            den = jnp.where(iota((TOK, 1), 0) < bound, d_den, 0.0)
            saved = pl.ds(room + j * TOK, width)
            s_high, s_low = halves(slopes(pair, den, base_s[:, saved], values(j, wide)))
            allowed = iota((1, width), 1) + j * TOK >= before
            keep = jnp.where(allowed, 1.0, 0.0)
            key = keys(j, wide) * keep.astype(BF16)
            dv_s[:, lanes] += keep * (nn(pair_t, high_s[:, saved]) + nn(pair_t, low_s[:, saved]))
            dk_s[:, lanes] += keep * (nn(query_t, s_high) + nn(query_t, s_low))
            dq_s[i] += nt(key, s_high) + nt(key, s_low)

        spans(i, backward)
        yield

    if count <= UNROLLED:
        rows = [row_block(i) for i in range(count)]
        for _ in range(2):
            for row in rows:
                next(row)
    else:
        each(0, count, lambda i: list(row_block(i)))

    for partner, out in zip(senders, outs):
        j = me ^ partner
        lanes = pl.ds(pl.multiple_of(j * TOK, TOK), TOK)
        total = dv_s[0:DV, lanes] + dv_s[DV : 2 * DV, lanes]
        out[0:TOK, 0:DV] = total.T.astype(BF16)
        back = taps[0:1] * mixed_grads[0, pl.ds(pl.multiple_of(j * TOK, TOK), TOK)]
        for shift in range(1, CONV):
            window = mixed_grads[shift, pl.ds(pl.multiple_of(j * TOK, TOK), TOK + 8)]
            back += taps[shift : shift + 1] * window[shift : shift + TOK]
        out[0:TOK, DV : 2 * DV] = back.astype(BF16)
        out[TOK : TOK + F] = (0.5 * dq_s[j]).astype(BF16)
        out[TOK + F : TOK + 2 * F] = dk_s[:, lanes].astype(BF16)


def attend(count, phase, bounds, taps, packed, grads):
    def in_order(blocks):
        return [blocks[partner] for partner in far_first(count)] if blocks else []

    outs = len(senders_of(count))
    saved = (count * (count - 1) // 2 if count <= UNROLLED else count - 1) * TOK
    return pl.pallas_call(
        functools.partial(attend_kernel, count, phase),
        cost_estimate=cost(5),
        out_shape=[jax.ShapeDtypeStruct((ROWS, 2 * DV), BF16)] * outs,
        in_specs=[SMEM, VMEM] + [VMEM] * (len(packed) + len(grads)),
        out_specs=[VMEM] * outs,
        scratch_shapes=[
            pltpu.VMEM((count, ROWS, 2 * DV), BF16),
            pltpu.VMEM((count, TOK, DV), BF16),
            pltpu.VMEM((count * TOK + 8, DV), F32),
            pltpu.VMEM((CONV, count * TOK + 8, DV), F32),
            pltpu.VMEM((TOK, saved), BF16),
            pltpu.VMEM((TOK, saved), BF16),
            pltpu.VMEM((TOK, saved), F32),
            pltpu.VMEM((count, TOK, 2 * DV), F32),
            pltpu.VMEM((count, F, TOK), F32),
            pltpu.VMEM((F, count * TOK), F32),
            pltpu.VMEM((2 * DV, count * TOK), F32),
        ],
        compiler_params=params(count),
    )(bounds, taps, *in_order(packed), *in_order(grads))


def unpack_kernel(count, phase, *rest):
    senders = senders_of(count)
    many = len(senders)
    me = lax.axis_index("ctx")
    last = phase == phases_of(count) - 1
    arrived, rest = rest[:many], rest[many:]
    earlier = None
    if phase > 0:
        earlier, rest = rest[0], rest[3:]
    v_ref, gate_ref = rest[:2]
    if last:
        rows_ref, flat_ref, sem_flat, sem = rest[4:]
    else:
        rows_ref, sem = rest[2:]
    copies = []
    for n, partner in enumerate(senders):
        head = first_head(me ^ partner, count) + phase
        lanes = pl.ds(pl.multiple_of(head * DV, DV), DV)
        copies.append((arrived[n].at[0:TOK, 0:DV], v_ref.at[0, :, lanes]))
        copies.append((arrived[n].at[0:TOK, DV : 2 * DV], gate_ref.at[0, :, lanes]))
    copies = [pltpu.make_async_copy(a, b, sem.at[n]) for n, (a, b) in enumerate(copies)]
    for copy in copies:
        copy.start()
    if earlier is not None:
        rows_ref[...] = earlier[...]
    for n, partner in enumerate(senders):
        head = first_head(me ^ partner, count) + phase
        rows = pl.ds(pl.multiple_of(head * F, F), F)
        for side in range(2):
            rows_ref[side, rows] = arrived[n][TOK + side * F : TOK + (side + 1) * F]
    if last:
        for side, ref in enumerate(rest[2:4]):
            flat_ref[side] = rows_ref[side].astype(F32).T.astype(BF16)
            copies.append(pltpu.make_async_copy(flat_ref.at[side], ref.at[0], sem_flat.at[side]))
            copies[-1].start()
    for copy in copies:
        copy.wait()


def unpack(count, phase, arrived, begun):
    wide = jax.ShapeDtypeStruct((1, TOK, HEADS * DV), BF16)
    narrow = jax.ShapeDtypeStruct((1, TOK, HEADS * F), BF16)
    turned = (2, HEADS * F, TOK)
    last = phase == phases_of(count) - 1
    many = len(arrived)
    small = [narrow, narrow] if last else [jax.ShapeDtypeStruct(turned, BF16)]
    return pl.pallas_call(
        functools.partial(unpack_kernel, count, phase),
        cost_estimate=cost(1),
        out_shape=[wide, wide] + small,
        in_specs=[VMEM] * many + [VMEM, HBM, HBM][: len(begun)],
        out_specs=[HBM] * 4 if last else [HBM, HBM, VMEM],
        input_output_aliases={many + 1: 0, many + 2: 1} if begun else {},
        scratch_shapes=(
            [
                pltpu.VMEM(turned, BF16),
                pltpu.VMEM((2, TOK, HEADS * F), BF16),
                pltpu.SemaphoreType.DMA((2,)),
            ]
            if last
            else []
        )
        + [pltpu.SemaphoreType.DMA((2 * many,))],
        compiler_params=params(count),
    )(*arrived, *begun)


def on_device(count, sections, q_in, k_in, v_in, gate_in, out_grad, conv_weight, bounds):
    phases, senders = phases_of(count), senders_of(count)

    def across(value, partner):
        if partner == 0:
            return value
        return lax.ppermute(value, "ctx", [(c, c ^ partner) for c in range(count)])

    def across_back(value, partner):
        pairs = [
            (c * sections + s, (c ^ partner) * sections + (s - 1) % sections)
            for c in range(count)
            for s in range(sections)
        ]
        return lax.ppermute(value, ("ctx", "pipe"), pairs)

    order = far_first(count)
    shift = [(s, (s - 1) % sections) for s in range(sections)]
    cotangent = lax.ppermute(out_grad, "pipe", shift)

    def spread(packed):
        moved = {partner: across(packed[partner], partner) for partner in order}
        return [moved[partner] for partner in range(count)]

    inputs = (q_in, k_in, v_in, gate_in)
    blocks = [spread(pack(count, 0, *inputs))]
    own_grads = pack_grads(count, cotangent)
    grads = spread(own_grads)
    for phase in range(1, phases):
        before = [own_grads[0]]
        blocks.append(spread(pack(count, phase, *inputs, cotangent, *before)))
    arrived = []
    for phase in range(phases):
        results = attend(count, phase, bounds, conv_weight, blocks[phase], grads)
        grads = []
        results = dict(zip(senders, results))
        moved = {p: across_back(results[p], p) for p in order if p in results}
        arrived.append([moved[partner] for partner in senders])
    begun = ()
    for phase in range(phases):
        out = unpack(count, phase, arrived[phase], begun)
        begun = (out[2], out[0], out[1])
    v_grad, gate_grad, q_grad, k_grad = out
    return q_grad, k_grad, v_grad, gate_grad


def solution(mesh):
    count, sections = mesh.shape["ctx"], mesh.shape["pipe"]
    split = P("pipe", "ctx", None)
    in_specs = (split,) * 5 + (P("pipe", None, None), P("pipe", None))
    return jax.shard_map(
        functools.partial(on_device, count, sections),
        mesh=mesh,
        in_specs=in_specs,
        out_specs=(split,) * 4,
        check_vma=False,
    )
```

```python
import functools

import jax
import jax.numpy as jnp
from jax import lax
from jax.experimental import pallas as pl
from jax.experimental.pallas import tpu as pltpu
from jax.sharding import PartitionSpec as P

HEADS = 8
F = 16
DV = 128
CONV = 3
TOK = 256
ROWS = TOK + 2 * F
BF16 = jnp.bfloat16
F32 = jnp.float32
UNROLLED = 4
HBM = pl.BlockSpec(memory_space=pltpu.HBM)

ANY = pl.BlockSpec(memory_space=pl.ANY)
SMEM = pl.BlockSpec(memory_space=pltpu.SMEM)
VMEM = pl.BlockSpec(memory_space=pltpu.VMEM)


def params(count):
    return pltpu.CompilerParams(vmem_limit_bytes=(14 if count <= UNROLLED else 44) * 1024 * 1024)


PACK_PARAMS = pltpu.CompilerParams(vmem_limit_bytes=125 * 512 * 1024)


def first_head(place, count):
    return (place * HEADS) // count


def cost(micros):
    return pl.CostEstimate(flops=int(1e9 * micros), bytes_accessed=int(3e6 * micros), transcendentals=0)


def lanes_of(head, width):
    return pl.ds(pl.multiple_of(head * width, width), width)


def phases_of(count):
    return max(1, HEADS // count)


def far_first(count):
    return sorted(range(count), key=lambda partner: -bin(partner).count("1"))


def senders_of(count, phase):
    order = far_first(count)
    if phase == phases_of(count) - 1:
        order = order[:1] + order[-1:] + order[1:-1]
    return [partner for partner in order if partner % max(1, count // HEADS) == 0]


def pack_kernel(count, phase, q_ref, k_ref, v_ref, gate_ref, *rest):
    me = lax.axis_index("ctx")
    packed = rest[-4 - count : -4]
    rows, turned, sem, sem_rows = rest[-4:]
    copies = []
    for partner, out in enumerate(packed):
        lanes = lanes_of(first_head(me ^ partner, count) + phase, DV)
        copies.append((v_ref.at[0, :, lanes], out.at[0:TOK, 0:DV]))
        copies.append((gate_ref.at[0, :, lanes], out.at[0:TOK, DV : 2 * DV]))
    copies = [pltpu.make_async_copy(a, b, sem.at[n]) for n, (a, b) in enumerate(copies)]
    loads = [
        pltpu.make_async_copy(ref.at[0], rows.at[side], sem_rows.at[side])
        for side, ref in enumerate((q_ref, k_ref))
    ]
    for copy in loads + copies:
        copy.start()
    for side, copy in enumerate(loads):
        copy.wait()
        turned[side] = rows[side].astype(F32).T.astype(BF16)
    for partner, out in enumerate(packed):
        head = first_head(me ^ partner, count) + phase
        for side in range(2):
            mine = turned[side, lanes_of(head, F)]
            out[TOK + side * F : TOK + (side + 1) * F] = mine
    if phase > 0:
        grad_ref = rest[0]
        for partner, out in enumerate(packed):
            pack_grad(count, phase, me ^ partner, grad_ref, out)
    for copy in copies:
        copy.wait()


def pack_grad(count, phase, place, grad_ref, out):
    mine = grad_ref[0, :, lanes_of(first_head(place, count) + phase, DV)]
    half = TOK // 2
    base = 0 if phase == 0 else ROWS
    out[base : base + half, 0:DV] = mine[0:half]
    out[base : base + half, DV : 2 * DV] = mine[half:TOK]


def pack(count, phase, q_in, k_in, v_in, gate_in, *others):
    rows = ROWS if phase == 0 else ROWS + TOK // 2
    return pl.pallas_call(
        functools.partial(pack_kernel, count, phase),
        cost_estimate=cost(2),
        out_shape=[jax.ShapeDtypeStruct((rows, 2 * DV), BF16)] * count,
        in_specs=[HBM] * 4 + [VMEM] * min(1, len(others)) + [ANY] * max(0, len(others) - 1),
        out_specs=[VMEM] * count,
        scratch_shapes=[
            pltpu.VMEM((2, TOK, HEADS * F), BF16),
            pltpu.VMEM((2, HEADS * F, TOK), BF16),
            pltpu.SemaphoreType.DMA((2 * count,)),
            pltpu.SemaphoreType.DMA((2,)),
        ],
        compiler_params=PACK_PARAMS if phase == 0 else params(count),
    )(q_in, k_in, v_in, gate_in, *others)


def pack_grads_kernel(count, grad_ref, *outs):
    outs = outs[-count:]
    me = lax.axis_index("ctx")
    for partner, out in enumerate(outs):
        pack_grad(count, 0, me ^ partner, grad_ref, out)


def pack_grads(count, grad, *before):
    return pl.pallas_call(
        functools.partial(pack_grads_kernel, count),
        cost_estimate=cost(0.5),
        out_shape=[jax.ShapeDtypeStruct((TOK // 2, 2 * DV), BF16)] * count,
        in_specs=[VMEM] + [ANY] * len(before),
        out_specs=[VMEM] * count,
        compiler_params=params(count),
    )(grad, *before)


def nn(a, b):
    return lax.dot_general(a, b, (((1,), (0,)), ((), ())), preferred_element_type=F32)


def nt(a, b):
    return lax.dot_general(a, b, (((1,), (1,)), ((), ())), preferred_element_type=F32)


def halves(x):
    high = x.astype(BF16)
    return high, (x - high.astype(F32)).astype(BF16)


def iota(shape, dim):
    return lax.broadcasted_iota(jnp.int32, shape, dim)


def each(low, high, body):
    if isinstance(low, int) and isinstance(high, int) and high - low <= UNROLLED:
        for step in range(low, high):
            body(step)
    else:

        def one(step, carry):
            body(step)
            return carry

        lax.fori_loop(low, high, one, 0)


def attend_kernel(count, phase, bounds, taps_ref, *rest):
    senders = senders_of(count, phase)
    packed, rest = dict(zip(far_first(count), rest)), rest[count:]
    grads, base = packed, ROWS
    if phase == 0:
        grads, base, rest = dict(zip(far_first(count), rest)), 0, rest[count:]
    outs = rest[: len(senders)]
    (block, grad, gates, mixed_grads, high_s, low_s, base_s, num_s, dq_s, dk_s, dv_s,
    ) = rest[len(senders) :]
    me = lax.axis_index("ctx")
    for partner in range(count):
        block[me ^ partner] = packed[partner][0:ROWS]
        for half in range(2):
            grad[me ^ partner, half * TOK // 2 : (half + 1) * TOK // 2] = grads[partner][
                base : base + TOK // 2, half * DV : (half + 1) * DV
            ]
    head = first_head(me, count) + phase
    taps = taps_ref[0, :, pl.ds(pl.multiple_of(head * DV, DV), DV)].astype(F32)
    gates[0:8] = jnp.zeros((8, DV), F32)
    mixed_grads[:, count * TOK : count * TOK + 8] = jnp.zeros((CONV, 8, DV), F32)

    def spread(j):
        gates[pl.ds(8 + j * TOK, TOK)] = block[j, 0:TOK, DV : 2 * DV].astype(F32)

    each(0, count, spread)

    def opening(i):
        bound = bounds[0, i]
        return jnp.where(bound < TOK, i * TOK + bound, 0)

    def earlier(i):
        if isinstance(i, int):
            last = jnp.int32(0)
            for j in range(i):
                last = jnp.maximum(last, opening(j))
            return last
        return lax.fori_loop(0, i, lambda j, last: jnp.maximum(last, opening(j)), jnp.int32(0))

    def values(j, wide):
        return block[pl.ds(j, wide), 0:TOK, 0:DV].reshape(wide * TOK, DV)

    def keys(j, wide):
        parts = [block[j + step, TOK + F : TOK + 2 * F] for step in range(wide)]
        return parts[0] if wide == 1 else jnp.concatenate(parts, axis=1)

    def spans(i, body):
        if isinstance(i, int):
            for j in range(i):
                body(j, 1)
        else:
            each(0, i, lambda j: body(j, 1))

    waiting = []

    def finish_waiting():
        while waiting:
            waiting.pop(0)()

    def ahead(first, second):
        found = first()
        finish_waiting()
        waiting.append(lambda: second(found))
        if count > UNROLLED:
            finish_waiting()

    def row_block(i):
        bound = bounds[0, i]
        before = earlier(i)
        row, col = iota((TOK, TOK), 0), iota((TOK, TOK), 1)
        same = (col <= row) & ((col >= bound) | (row < bound))
        query_t = block[i, TOK : TOK + F] * BF16(0.25)
        query = query_t.astype(F32).T.astype(BF16)
        query_t = query_t * BF16(2)

        def kernel_of(j, wide):
            base = 1.0 + nn(query, keys(j, wide))
            return base, base * base + 1.0

        def weigh(high, low, value):
            value = jnp.concatenate([value, jnp.ones_like(value)], axis=1)
            return nn(high, value) + nn(low, value)

        kept = {}

        def own_forward(found):
            kept["base"], kern = found
            kept["high"], kept["low"] = halves(jnp.where(same, kern, 0.0))
            kept["sum"] = weigh(kept["high"], kept["low"], values(i, 1))

        ahead(lambda: kernel_of(i, 1), own_forward)
        num_s[i] = jnp.zeros((TOK, 2 * DV), F32)
        room = (i * (i - 1)) // 2 * TOK if isinstance(i, int) else 0

        def forward(j, wide):
            width = wide * TOK

            def weigh_older(found):
                base, kern = found
                high, low = halves(kern)
                lanes = pl.ds(room + j * TOK, width)
                base_s[:, lanes] = base
                high_s[:, lanes] = high
                low_s[:, lanes] = low
                value = values(j, wide)
                allowed = iota((width, DV), 0) + j * TOK >= before
                ones = jnp.where(allowed, 1.0, 0.0).astype(BF16)
                value = jnp.concatenate([value * ones, ones], axis=1)
                num_s[i] += nn(high, value) + nn(low, value)

            ahead(lambda: kernel_of(j, wide), weigh_older)

        spans(i, forward)
        yield
        old = iota((TOK, 2 * DV), 0) < bound
        total = kept["sum"] + jnp.where(old, num_s[i], 0.0)
        num, den = total[:, 0:DV], total[:, DV:]

        position = iota((TOK, DV), 0) + i * TOK
        depth = position - jnp.where(iota((TOK, DV), 0) >= bound, opening(i), before)
        mixed = taps[0:1] * gates[pl.ds(8 + i * TOK, TOK)]
        for shift in range(1, CONV):
            moved = gates[pl.ds(8 - shift + i * TOK, TOK)]
            mixed += jnp.where(depth >= shift, taps[shift : shift + 1] * moved, 0.0)
        incoming = grad[i].astype(F32)
        gate = 1.0 / (1.0 + jnp.exp(-mixed))
        scale = 1.0 / den
        attended = num * scale
        d_num = incoming * mixed * gate * scale
        d_den = -jnp.sum(d_num * attended, axis=1, keepdims=True)
        mixed_grad = incoming * attended * gate * (1.0 + mixed * (1.0 - gate))
        mixed_grads[0, pl.ds(i * TOK, TOK)] = mixed_grad
        for shift in range(1, CONV):
            mixed_grads[shift, pl.ds(i * TOK, TOK)] = jnp.where(depth >= shift, mixed_grad, 0.0)

        d_pair = jnp.concatenate(halves(d_num), axis=1)
        d_pair_t = jnp.concatenate(halves(d_num.T), axis=0)

        def slopes(d_pair, d_den, base, value):
            return (nt(d_pair, jnp.concatenate([value, value], axis=1)) + d_den) * base

        def own_slopes():
            slope = slopes(d_pair, d_den, kept["base"], values(i, 1))
            return halves(jnp.where(same, slope, 0.0))

        def own_backward(found):
            s_high, s_low = found
            key = keys(i, 1)
            lanes = pl.ds(i * TOK, TOK)
            dv_s[:, lanes] = nn(d_pair_t, kept["high"]) + nn(d_pair_t, kept["low"])
            dk_s[:, lanes] = nn(query_t, s_high) + nn(query_t, s_low)
            dq_s[i] = nt(key, s_high) + nt(key, s_low)

        ahead(own_slopes, own_backward)

        def backward(j, wide):
            width = wide * TOK
            lanes = pl.ds(j * TOK, width)
            saved = pl.ds(room + j * TOK, width)

            def older_slopes():
                row_old = jnp.where(old, 1.0, 0.0).astype(BF16)
                den = jnp.where(iota((TOK, 1), 0) < bound, d_den, 0.0)
                return halves(slopes(d_pair * row_old, den, base_s[:, saved], values(j, wide)))

            def older_backward(found):
                s_high, s_low = found
                lane_old = jnp.where(iota((2 * DV, TOK), 1) < bound, 1.0, 0.0).astype(BF16)
                pair_t = d_pair_t * lane_old
                keep = jnp.where(iota((1, width), 1) + j * TOK >= before, 1.0, 0.0)
                key = keys(j, wide) * keep.astype(BF16)
                dv_s[:, lanes] += keep * (
                    nn(pair_t, high_s[:, saved]) + nn(pair_t, low_s[:, saved])
                )
                dk_s[:, lanes] += keep * (nn(query_t, s_high) + nn(query_t, s_low))
                dq_s[i] += nt(key, s_high) + nt(key, s_low)

            ahead(older_slopes, older_backward)

        spans(i, backward)
        yield

    if count <= UNROLLED:
        rows = [row_block(i) for i in range(count)]
        for _ in range(2):
            for row in rows:
                next(row)
            finish_waiting()
    else:
        each(0, count, lambda i: list(row_block(i)))

    for partner, out in zip(senders, outs):
        j = me ^ partner
        lanes = pl.ds(pl.multiple_of(j * TOK, TOK), TOK)
        total = dv_s[0:DV, lanes] + dv_s[DV : 2 * DV, lanes]
        out[0:TOK, 0:DV] = total.T.astype(BF16)
        back = taps[0:1] * mixed_grads[0, pl.ds(pl.multiple_of(j * TOK, TOK), TOK)]
        for shift in range(1, CONV):
            window = mixed_grads[shift, pl.ds(pl.multiple_of(j * TOK, TOK), TOK + 8)]
            back += taps[shift : shift + 1] * window[shift : shift + TOK]
        out[0:TOK, DV : 2 * DV] = back.astype(BF16)
        out[TOK : TOK + F] = (0.5 * dq_s[j]).astype(BF16)
        out[TOK + F : TOK + 2 * F] = dk_s[:, lanes].astype(BF16)


def attend(count, phase, bounds, taps, packed, grads):
    def in_order(blocks):
        return [blocks[partner] for partner in far_first(count)] if blocks else []

    outs = len(senders_of(count, phase))
    saved = (count * (count - 1) // 2 if count <= UNROLLED else count - 1) * TOK
    return pl.pallas_call(
        functools.partial(attend_kernel, count, phase),
        cost_estimate=cost(5),
        out_shape=[jax.ShapeDtypeStruct((ROWS, 2 * DV), BF16)] * outs,
        in_specs=[SMEM, VMEM] + [VMEM] * (len(packed) + len(grads)),
        out_specs=[VMEM] * outs,
        scratch_shapes=[
            pltpu.VMEM((count, ROWS, 2 * DV), BF16),
            pltpu.VMEM((count, TOK, DV), BF16),
            pltpu.VMEM((count * TOK + 8, DV), F32),
            pltpu.VMEM((CONV, count * TOK + 8, DV), F32),
            pltpu.VMEM((TOK, saved), BF16),
            pltpu.VMEM((TOK, saved), BF16),
            pltpu.VMEM((TOK, saved), F32),
            pltpu.VMEM((count, TOK, 2 * DV), F32),
            pltpu.VMEM((count, F, TOK), F32),
            pltpu.VMEM((F, count * TOK), F32),
            pltpu.VMEM((2 * DV, count * TOK), F32),
        ],
        compiler_params=params(count),
    )(bounds, taps, *in_order(packed), *in_order(grads))


def unpack_kernel(count, phase, *rest):
    senders = senders_of(count, phase)
    many = len(senders)
    me = lax.axis_index("ctx")
    last = phase == phases_of(count) - 1
    arrived, rest = rest[:many], rest[many:]
    earlier = None
    if phase > 0:
        earlier, rest = rest[0], rest[3:]
    v_ref, gate_ref = rest[:2]
    if last:
        rows_ref, flat_ref, sem_flat, sem = rest[4:]
    else:
        rows_ref, sem = rest[2:]
    copies = []
    for n, partner in enumerate(senders):
        head = first_head(me ^ partner, count) + phase
        lanes = pl.ds(pl.multiple_of(head * DV, DV), DV)
        copies.append((arrived[n].at[0:TOK, 0:DV], v_ref.at[0, :, lanes]))
        copies.append((arrived[n].at[0:TOK, DV : 2 * DV], gate_ref.at[0, :, lanes]))
    copies = [pltpu.make_async_copy(a, b, sem.at[n]) for n, (a, b) in enumerate(copies)]
    for copy in copies:
        copy.start()
    if earlier is not None:
        rows_ref[...] = earlier[...]
    for n, partner in enumerate(senders):
        head = first_head(me ^ partner, count) + phase
        rows = pl.ds(pl.multiple_of(head * F, F), F)
        for side in range(2):
            rows_ref[side, rows] = arrived[n][TOK + side * F : TOK + (side + 1) * F]
    if last:
        for side, ref in enumerate(rest[2:4]):
            flat_ref[side] = rows_ref[side].astype(F32).T.astype(BF16)
            copies.append(pltpu.make_async_copy(flat_ref.at[side], ref.at[0], sem_flat.at[side]))
            copies[-1].start()
    for copy in copies:
        copy.wait()


def unpack(count, phase, arrived, begun):
    wide = jax.ShapeDtypeStruct((1, TOK, HEADS * DV), BF16)
    narrow = jax.ShapeDtypeStruct((1, TOK, HEADS * F), BF16)
    turned = (2, HEADS * F, TOK)
    last = phase == phases_of(count) - 1
    many = len(arrived)
    small = [narrow, narrow] if last else [jax.ShapeDtypeStruct(turned, BF16)]
    return pl.pallas_call(
        functools.partial(unpack_kernel, count, phase),
        cost_estimate=cost(1),
        out_shape=[wide, wide] + small,
        in_specs=[VMEM] * many + [VMEM, HBM, HBM][: len(begun)],
        out_specs=[HBM] * 4 if last else [HBM, HBM, VMEM],
        input_output_aliases={many + 1: 0, many + 2: 1} if begun else {},
        scratch_shapes=(
            [
                pltpu.VMEM(turned, BF16),
                pltpu.VMEM((2, TOK, HEADS * F), BF16),
                pltpu.SemaphoreType.DMA((2,)),
            ]
            if last
            else []
        )
        + [pltpu.SemaphoreType.DMA((2 * many,))],
        compiler_params=params(count),
    )(*arrived, *begun)


def on_device(count, sections, q_in, k_in, v_in, gate_in, out_grad, conv_weight, bounds):
    phases = phases_of(count)

    def across(value, partner):
        if partner == 0:
            return value
        return lax.ppermute(value, "ctx", [(c, c ^ partner) for c in range(count)])

    def across_back(value, partner):
        pairs = [
            (c * sections + s, (c ^ partner) * sections + (s - 1) % sections)
            for c in range(count)
            for s in range(sections)
        ]
        return lax.ppermute(value, ("ctx", "pipe"), pairs)

    order = far_first(count)
    shift = [(s, (s - 1) % sections) for s in range(sections)]
    cotangent = lax.ppermute(out_grad, "pipe", shift)

    def spread(packed):
        moved = {partner: across(packed[partner], partner) for partner in order}
        return [moved[partner] for partner in range(count)]

    inputs = (q_in, k_in, v_in, gate_in)
    blocks = [spread(pack(count, 0, *inputs))]
    own_grads = pack_grads(count, cotangent)
    grads = spread(own_grads)
    for phase in range(1, phases):
        before = [own_grads[0]]
        blocks.append(spread(pack(count, phase, *inputs, cotangent, *before)))
    arrived = []
    for phase in range(phases):
        results = attend(count, phase, bounds, conv_weight, blocks[phase], grads)
        grads = []
        senders = senders_of(count, phase)
        results = dict(zip(senders, results))
        moved = {p: across_back(results[p], p) for p in order if p in results}
        arrived.append([moved[partner] for partner in senders])
    begun = ()
    for phase in range(phases):
        out = unpack(count, phase, arrived[phase], begun)
        begun = (out[2], out[0], out[1])
    v_grad, gate_grad, q_grad, k_grad = out
    return q_grad, k_grad, v_grad, gate_grad


def solution(mesh):
    count, sections = mesh.shape["ctx"], mesh.shape["pipe"]
    split = P("pipe", "ctx", None)
    in_specs = (split,) * 5 + (P("pipe", None, None), P("pipe", None))
    return jax.shard_map(
        functools.partial(on_device, count, sections),
        mesh=mesh,
        in_specs=in_specs,
        out_specs=(split,) * 4,
        check_vma=False,
    )
```

```python
import functools

import jax
import jax.numpy as jnp
from jax import lax
from jax.experimental import pallas as pl
from jax.experimental.pallas import tpu as pltpu
from jax.sharding import PartitionSpec as P

HEADS = 8
F = 16
DV = 128
CONV = 3
TOK = 256
ROWS = TOK + 2 * F
BF16 = jnp.bfloat16
F32 = jnp.float32
UNROLLED = 4
HBM = pl.BlockSpec(memory_space=pltpu.HBM)

ANY = pl.BlockSpec(memory_space=pl.ANY)
SMEM = pl.BlockSpec(memory_space=pltpu.SMEM)
VMEM = pl.BlockSpec(memory_space=pltpu.VMEM)


def params(count):
    return pltpu.CompilerParams(vmem_limit_bytes=(14 if count <= UNROLLED else 44) * 1024 * 1024)


PACK_PARAMS = pltpu.CompilerParams(vmem_limit_bytes=125 * 512 * 1024)


def first_head(place, count):
    return (place * HEADS) // count


def cost(micros):
    return pl.CostEstimate(flops=int(1e9 * micros), bytes_accessed=int(3e6 * micros), transcendentals=0)


def lanes_of(head, width):
    return pl.ds(pl.multiple_of(head * width, width), width)


def phases_of(count):
    return max(1, HEADS // count)


def far_first(count):
    return sorted(range(count), key=lambda partner: -bin(partner).count("1"))


def senders_of(count, phase):
    order = far_first(count)
    if phase == phases_of(count) - 1:
        order = order[:1] + order[-1:] + order[1:-1]
    return [partner for partner in order if partner % max(1, count // HEADS) == 0]


def pack_kernel(count, phase, q_ref, k_ref, v_ref, gate_ref, *rest):
    me = lax.axis_index("ctx")
    packed = rest[-4 - count : -4]
    rows, turned, sem, sem_rows = rest[-4:]
    copies = []
    for partner, out in enumerate(packed):
        lanes = lanes_of(first_head(me ^ partner, count) + phase, DV)
        copies.append((v_ref.at[0, :, lanes], out.at[0:TOK, 0:DV]))
        copies.append((gate_ref.at[0, :, lanes], out.at[0:TOK, DV : 2 * DV]))
    copies = [pltpu.make_async_copy(a, b, sem.at[n]) for n, (a, b) in enumerate(copies)]
    loads = [
        pltpu.make_async_copy(ref.at[0], rows.at[side], sem_rows.at[side])
        for side, ref in enumerate((q_ref, k_ref))
    ]
    for copy in loads + copies:
        copy.start()
    for side, copy in enumerate(loads):
        copy.wait()
        turned[side] = rows[side].astype(F32).T.astype(BF16)
    for partner, out in enumerate(packed):
        head = first_head(me ^ partner, count) + phase
        for side in range(2):
            mine = turned[side, lanes_of(head, F)]
            out[TOK + side * F : TOK + (side + 1) * F] = mine
    if phase > 0:
        grad_ref = rest[0]
        for partner, out in enumerate(packed):
            pack_grad(count, phase, me ^ partner, grad_ref, out)
    for copy in copies:
        copy.wait()


def pack_grad(count, phase, place, grad_ref, out):
    mine = grad_ref[0, :, lanes_of(first_head(place, count) + phase, DV)]
    half = TOK // 2
    base = 0 if phase == 0 else ROWS
    out[base : base + half, 0:DV] = mine[0:half]
    out[base : base + half, DV : 2 * DV] = mine[half:TOK]


def pack(count, phase, q_in, k_in, v_in, gate_in, *others):
    rows = ROWS if phase == 0 else ROWS + TOK // 2
    return pl.pallas_call(
        functools.partial(pack_kernel, count, phase),
        cost_estimate=cost(2),
        out_shape=[jax.ShapeDtypeStruct((rows, 2 * DV), BF16)] * count,
        in_specs=[HBM] * 4 + [VMEM] * min(1, len(others)) + [ANY] * max(0, len(others) - 1),
        out_specs=[VMEM] * count,
        scratch_shapes=[
            pltpu.VMEM((2, TOK, HEADS * F), BF16),
            pltpu.VMEM((2, HEADS * F, TOK), BF16),
            pltpu.SemaphoreType.DMA((2 * count,)),
            pltpu.SemaphoreType.DMA((2,)),
        ],
        compiler_params=PACK_PARAMS if phase == 0 else params(count),
    )(q_in, k_in, v_in, gate_in, *others)


def pack_grads_kernel(count, grad_ref, *outs):
    outs = outs[-count:]
    me = lax.axis_index("ctx")
    for partner, out in enumerate(outs):
        pack_grad(count, 0, me ^ partner, grad_ref, out)


def pack_grads(count, grad, *before):
    return pl.pallas_call(
        functools.partial(pack_grads_kernel, count),
        cost_estimate=cost(0.5),
        out_shape=[jax.ShapeDtypeStruct((TOK // 2, 2 * DV), BF16)] * count,
        in_specs=[VMEM] + [ANY] * len(before),
        out_specs=[VMEM] * count,
        compiler_params=params(count),
    )(grad, *before)


def nn(a, b):
    return lax.dot_general(a, b, (((1,), (0,)), ((), ())), preferred_element_type=F32)


def nt(a, b):
    return lax.dot_general(a, b, (((1,), (1,)), ((), ())), preferred_element_type=F32)


def halves(x):
    high = x.astype(BF16)
    return high, (x - high.astype(F32)).astype(BF16)


def iota(shape, dim):
    return lax.broadcasted_iota(jnp.int32, shape, dim)


def each(low, high, body):
    if isinstance(low, int) and isinstance(high, int) and high - low <= UNROLLED:
        for step in range(low, high):
            body(step)
    else:

        def one(step, carry):
            body(step)
            return carry

        lax.fori_loop(low, high, one, 0)


def attend_kernel(count, phase, bounds, taps_ref, *rest):
    senders = senders_of(count, phase)
    packed, rest = dict(zip(far_first(count), rest)), rest[count:]
    grads, base = packed, ROWS
    if phase == 0:
        grads, base, rest = dict(zip(far_first(count), rest)), 0, rest[count:]
    outs = rest[: len(senders)]
    (block, grad, gates, mixed_grads, high_s, low_s, base_s, num_s, dq_s, dk_s, dv_s,
    ) = rest[len(senders) :]
    me = lax.axis_index("ctx")
    for partner in range(count):
        block[me ^ partner] = packed[partner][0:ROWS]
        for half in range(2):
            grad[me ^ partner, half * TOK // 2 : (half + 1) * TOK // 2] = grads[partner][
                base : base + TOK // 2, half * DV : (half + 1) * DV
            ]
    head = first_head(me, count) + phase
    taps = taps_ref[0, :, pl.ds(pl.multiple_of(head * DV, DV), DV)].astype(F32)
    gates[0:8] = jnp.zeros((8, DV), F32)
    mixed_grads[:, count * TOK : count * TOK + 8] = jnp.zeros((CONV, 8, DV), F32)

    def spread(j):
        gates[pl.ds(8 + j * TOK, TOK)] = block[j, 0:TOK, DV : 2 * DV].astype(F32)

    each(0, count, spread)

    def opening(i):
        bound = bounds[0, i]
        return jnp.where(bound < TOK, i * TOK + bound, 0)

    def earlier(i):
        if isinstance(i, int):
            last = jnp.int32(0)
            for j in range(i):
                last = jnp.maximum(last, opening(j))
            return last
        return lax.fori_loop(0, i, lambda j, last: jnp.maximum(last, opening(j)), jnp.int32(0))

    def values(j, wide):
        return block[pl.ds(j, wide), 0:TOK, 0:DV].reshape(wide * TOK, DV)

    def keys(j, wide):
        parts = [block[j + step, TOK + F : TOK + 2 * F] for step in range(wide)]
        return parts[0] if wide == 1 else jnp.concatenate(parts, axis=1)

    def spans(i, body):
        if isinstance(i, int):
            for j in range(i):
                body(j, 1)
        else:
            each(0, i, lambda j: body(j, 1))

    waiting = []

    def finish_waiting():
        while waiting:
            waiting.pop(0)()

    def ahead(first, second):
        found = first()
        finish_waiting()
        waiting.append(lambda: second(found))
        if count > UNROLLED:
            finish_waiting()

    def row_block(i):
        bound = bounds[0, i]
        before = earlier(i)
        row, col = iota((TOK, TOK), 0), iota((TOK, TOK), 1)
        same = (col <= row) & ((col >= bound) | (row < bound))
        query_t = block[i, TOK : TOK + F] * BF16(0.25)
        query = query_t.astype(F32).T.astype(BF16)
        query_t = query_t * BF16(2)

        def kernel_of(j, wide):
            base = 1.0 + nn(query, keys(j, wide))
            return base, base * base + 1.0

        def weigh(high, low, value):
            value = jnp.concatenate([value, jnp.ones_like(value)], axis=1)
            return nn(high, value) + nn(low, value)

        kept = {}

        def own_forward(found):
            kept["base"], kern = found
            kept["high"], kept["low"] = halves(jnp.where(same, kern, 0.0))
            kept["sum"] = weigh(kept["high"], kept["low"], values(i, 1))

        ahead(lambda: kernel_of(i, 1), own_forward)
        num_s[i] = jnp.zeros((TOK, 2 * DV), F32)
        room = (i * (i - 1)) // 2 * TOK if isinstance(i, int) else 0

        def forward(j, wide):
            width = wide * TOK

            def weigh_older(found):
                base, kern = found
                high, low = halves(kern)
                lanes = pl.ds(room + j * TOK, width)
                base_s[:, lanes] = base
                high_s[:, lanes] = high
                low_s[:, lanes] = low
                value = values(j, wide)
                allowed = iota((width, DV), 0) + j * TOK >= before
                ones = jnp.where(allowed, 1.0, 0.0).astype(BF16)
                value = jnp.concatenate([value * ones, ones], axis=1)
                num_s[i] += nn(high, value) + nn(low, value)

            ahead(lambda: kernel_of(j, wide), weigh_older)

        spans(i, forward)
        yield
        old = iota((TOK, 2 * DV), 0) < bound
        total = kept["sum"] + jnp.where(old, num_s[i], 0.0)
        num, den = total[:, 0:DV], total[:, DV:]

        position = iota((TOK, DV), 0) + i * TOK
        depth = position - jnp.where(iota((TOK, DV), 0) >= bound, opening(i), before)
        mixed = taps[0:1] * gates[pl.ds(8 + i * TOK, TOK)]
        for shift in range(1, CONV):
            moved = gates[pl.ds(8 - shift + i * TOK, TOK)]
            mixed += jnp.where(depth >= shift, taps[shift : shift + 1] * moved, 0.0)
        incoming = grad[i].astype(F32)
        spread_mixed = 1.0 + jnp.exp(-mixed)
        shared = 1.0 / (spread_mixed * den)
        gate, scale = shared * den, shared * spread_mixed
        attended = num * scale
        d_num = incoming * mixed * gate * scale
        d_den = -jnp.sum(d_num * attended, axis=1, keepdims=True)
        mixed_grad = incoming * attended * gate * (1.0 + mixed * (1.0 - gate))
        mixed_grads[0, pl.ds(i * TOK, TOK)] = mixed_grad
        for shift in range(1, CONV):
            mixed_grads[shift, pl.ds(i * TOK, TOK)] = jnp.where(depth >= shift, mixed_grad, 0.0)

        d_pair = jnp.concatenate(halves(d_num), axis=1)
        d_pair_t = jnp.concatenate(halves(d_num.T), axis=0)

        def slopes(d_pair, d_den, base, value):
            return (nt(d_pair, jnp.concatenate([value, value], axis=1)) + d_den) * base

        def own_slopes():
            slope = slopes(d_pair, d_den, kept["base"], values(i, 1))
            return halves(jnp.where(same, slope, 0.0))

        def own_backward(found):
            s_high, s_low = found
            key = keys(i, 1)
            lanes = pl.ds(i * TOK, TOK)
            dv_s[:, lanes] = nn(d_pair_t, kept["high"]) + nn(d_pair_t, kept["low"])
            dk_s[:, lanes] = nn(query_t, s_high) + nn(query_t, s_low)
            dq_s[i] = nt(key, s_high) + nt(key, s_low)

        ahead(own_slopes, own_backward)

        def backward(j, wide):
            width = wide * TOK
            lanes = pl.ds(j * TOK, width)
            saved = pl.ds(room + j * TOK, width)

            def older_slopes():
                row_old = jnp.where(old, 1.0, 0.0).astype(BF16)
                den = jnp.where(iota((TOK, 1), 0) < bound, d_den, 0.0)
                return halves(slopes(d_pair * row_old, den, base_s[:, saved], values(j, wide)))

            def older_backward(found):
                s_high, s_low = found
                lane_old = jnp.where(iota((2 * DV, TOK), 1) < bound, 1.0, 0.0).astype(BF16)
                pair_t = d_pair_t * lane_old
                keep = jnp.where(iota((1, width), 1) + j * TOK >= before, 1.0, 0.0)
                key = keys(j, wide) * keep.astype(BF16)
                dv_s[:, lanes] += keep * (
                    nn(pair_t, high_s[:, saved]) + nn(pair_t, low_s[:, saved])
                )
                dk_s[:, lanes] += keep * (nn(query_t, s_high) + nn(query_t, s_low))
                dq_s[i] += nt(key, s_high) + nt(key, s_low)

            ahead(older_slopes, older_backward)

        spans(i, backward)
        yield

    if count <= UNROLLED:
        rows = [row_block(i) for i in range(count)]
        for _ in range(2):
            for row in rows:
                next(row)
            finish_waiting()
    else:
        each(0, count, lambda i: list(row_block(i)))

    for partner, out in zip(senders, outs):
        j = me ^ partner
        lanes = pl.ds(pl.multiple_of(j * TOK, TOK), TOK)
        total = dv_s[0:DV, lanes] + dv_s[DV : 2 * DV, lanes]
        out[0:TOK, 0:DV] = total.T.astype(BF16)
        back = taps[0:1] * mixed_grads[0, pl.ds(pl.multiple_of(j * TOK, TOK), TOK)]
        for shift in range(1, CONV):
            window = mixed_grads[shift, pl.ds(pl.multiple_of(j * TOK, TOK), TOK + 8)]
            back += taps[shift : shift + 1] * window[shift : shift + TOK]
        out[0:TOK, DV : 2 * DV] = back.astype(BF16)
        out[TOK : TOK + F] = (0.5 * dq_s[j]).astype(BF16)
        out[TOK + F : TOK + 2 * F] = dk_s[:, lanes].astype(BF16)


def attend(count, phase, bounds, taps, packed, grads):
    def in_order(blocks):
        return [blocks[partner] for partner in far_first(count)] if blocks else []

    outs = len(senders_of(count, phase))
    saved = (count * (count - 1) // 2 if count <= UNROLLED else count - 1) * TOK
    return pl.pallas_call(
        functools.partial(attend_kernel, count, phase),
        cost_estimate=cost(5),
        out_shape=[jax.ShapeDtypeStruct((ROWS, 2 * DV), BF16)] * outs,
        in_specs=[SMEM, VMEM] + [VMEM] * (len(packed) + len(grads)),
        out_specs=[VMEM] * outs,
        scratch_shapes=[
            pltpu.VMEM((count, ROWS, 2 * DV), BF16),
            pltpu.VMEM((count, TOK, DV), BF16),
            pltpu.VMEM((count * TOK + 8, DV), F32),
            pltpu.VMEM((CONV, count * TOK + 8, DV), F32),
            pltpu.VMEM((TOK, saved), BF16),
            pltpu.VMEM((TOK, saved), BF16),
            pltpu.VMEM((TOK, saved), F32),
            pltpu.VMEM((count, TOK, 2 * DV), F32),
            pltpu.VMEM((count, F, TOK), F32),
            pltpu.VMEM((F, count * TOK), F32),
            pltpu.VMEM((2 * DV, count * TOK), F32),
        ],
        compiler_params=params(count),
    )(bounds, taps, *in_order(packed), *in_order(grads))


def unpack_kernel(count, phase, *rest):
    senders = senders_of(count, phase)
    many = len(senders)
    me = lax.axis_index("ctx")
    last = phase == phases_of(count) - 1
    arrived, rest = rest[:many], rest[many:]
    earlier = None
    if phase > 0:
        earlier, rest = rest[0], rest[3:]
    v_ref, gate_ref = rest[:2]
    if last:
        rows_ref, flat_ref, sem_flat, sem = rest[4:]
    else:
        rows_ref, sem = rest[2:]
    copies = []
    for n, partner in enumerate(senders):
        head = first_head(me ^ partner, count) + phase
        lanes = pl.ds(pl.multiple_of(head * DV, DV), DV)
        copies.append((arrived[n].at[0:TOK, 0:DV], v_ref.at[0, :, lanes]))
        copies.append((arrived[n].at[0:TOK, DV : 2 * DV], gate_ref.at[0, :, lanes]))
    copies = [pltpu.make_async_copy(a, b, sem.at[n]) for n, (a, b) in enumerate(copies)]
    for copy in copies:
        copy.start()
    if earlier is not None:
        rows_ref[...] = earlier[...]
    for n, partner in enumerate(senders):
        head = first_head(me ^ partner, count) + phase
        rows = pl.ds(pl.multiple_of(head * F, F), F)
        for side in range(2):
            rows_ref[side, rows] = arrived[n][TOK + side * F : TOK + (side + 1) * F]
    if last:
        for side, ref in enumerate(rest[2:4]):
            flat_ref[side] = rows_ref[side].astype(F32).T.astype(BF16)
            copies.append(pltpu.make_async_copy(flat_ref.at[side], ref.at[0], sem_flat.at[side]))
            copies[-1].start()
    for copy in copies:
        copy.wait()


def unpack(count, phase, arrived, begun):
    wide = jax.ShapeDtypeStruct((1, TOK, HEADS * DV), BF16)
    narrow = jax.ShapeDtypeStruct((1, TOK, HEADS * F), BF16)
    turned = (2, HEADS * F, TOK)
    last = phase == phases_of(count) - 1
    many = len(arrived)
    small = [narrow, narrow] if last else [jax.ShapeDtypeStruct(turned, BF16)]
    return pl.pallas_call(
        functools.partial(unpack_kernel, count, phase),
        cost_estimate=cost(1),
        out_shape=[wide, wide] + small,
        in_specs=[VMEM] * many + [VMEM, HBM, HBM][: len(begun)],
        out_specs=[HBM] * 4 if last else [HBM, HBM, VMEM],
        input_output_aliases={many + 1: 0, many + 2: 1} if begun else {},
        scratch_shapes=(
            [
                pltpu.VMEM(turned, BF16),
                pltpu.VMEM((2, TOK, HEADS * F), BF16),
                pltpu.SemaphoreType.DMA((2,)),
            ]
            if last
            else []
        )
        + [pltpu.SemaphoreType.DMA((2 * many,))],
        compiler_params=params(count),
    )(*arrived, *begun)


def on_device(count, sections, q_in, k_in, v_in, gate_in, out_grad, conv_weight, bounds):
    phases = phases_of(count)

    def across(value, partner):
        if partner == 0:
            return value
        return lax.ppermute(value, "ctx", [(c, c ^ partner) for c in range(count)])

    def across_back(value, partner):
        pairs = [
            (c * sections + s, (c ^ partner) * sections + (s - 1) % sections)
            for c in range(count)
            for s in range(sections)
        ]
        return lax.ppermute(value, ("ctx", "pipe"), pairs)

    order = far_first(count)
    shift = [(s, (s - 1) % sections) for s in range(sections)]
    cotangent = lax.ppermute(out_grad, "pipe", shift)

    def spread(packed):
        moved = {partner: across(packed[partner], partner) for partner in order}
        return [moved[partner] for partner in range(count)]

    inputs = (q_in, k_in, v_in, gate_in)
    blocks = [spread(pack(count, 0, *inputs))]
    own_grads = pack_grads(count, cotangent)
    grads = spread(own_grads)
    for phase in range(1, phases):
        before = [own_grads[0]]
        blocks.append(spread(pack(count, phase, *inputs, cotangent, *before)))
    arrived = []
    for phase in range(phases):
        results = attend(count, phase, bounds, conv_weight, blocks[phase], grads)
        grads = []
        senders = senders_of(count, phase)
        results = dict(zip(senders, results))
        moved = {p: across_back(results[p], p) for p in order if p in results}
        arrived.append([moved[partner] for partner in senders])
    begun = ()
    for phase in range(phases):
        out = unpack(count, phase, arrived[phase], begun)
        begun = (out[2], out[0], out[1])
    v_grad, gate_grad, q_grad, k_grad = out
    return q_grad, k_grad, v_grad, gate_grad


def solution(mesh):
    count, sections = mesh.shape["ctx"], mesh.shape["pipe"]
    split = P("pipe", "ctx", None)
    in_specs = (split,) * 5 + (P("pipe", None, None), P("pipe", None))
    return jax.shard_map(
        functools.partial(on_device, count, sections),
        mesh=mesh,
        in_specs=in_specs,
        out_specs=(split,) * 4,
        check_vma=False,
    )
```
